32 devices in a mesh: seq: 8 (over z, x), dp: 4 (over y, core).
Axes of the slice: x: 2, y: 2, z: 4, core: 2. Of those that a mesh axis runs over, the one named last changes fastest.
Arguments:
- tokens: bfloat16 [4, 2048, 1024], P('dp', 'seq'), may hold values from -6 to 6
- attn_gain: bfloat16 [1024], P(('seq', 'dp')), may hold values from 0.5 to 1.5
- q_weight: bfloat16 [1024, 1024], P(('seq', 'dp')), may hold values from -0.1875 to 0.1875
- k_weight: bfloat16 [1024, 512], P(('seq', 'dp')), may hold values from -0.1875 to 0.1875
- v_weight: bfloat16 [1024, 512], P(('seq', 'dp')), may hold values from -0.1875 to 0.1875
- q_norm_gain: bfloat16 [64], replicated, may hold values from 0.25 to 1.75
- k_norm_gain: bfloat16 [64], replicated, may hold values from 0.25 to 1.75
- o_weight: bfloat16 [1024, 1024], P(('seq', 'dp')), may hold values from -1 to 1
- ffn_gain: bfloat16 [1024], P(('seq', 'dp')), may hold values from 0.5 to 1.5
- gate_weight: bfloat16 [1024, 4608], P(('seq', 'dp')), may hold values from -0.1875 to 0.1875
- up_weight: bfloat16 [1024, 4608], P(('seq', 'dp')), may hold values from -0.1875 to 0.1875
- down_weight: bfloat16 [4608, 1024], P(('seq', 'dp')), may hold values from -0.09375 to 0.09375
- doc_lengths: int32 [4, 4], P('dp'), may hold values from 1 to 2048, as said below
- cotangent: bfloat16 [4, 2048, 1024], P('dp', 'seq'), may hold values from -6 to 6
Outputs:
- output: bfloat16 [4, 2048, 1024], P('dp', 'seq')
- input_grad: float32 [4, 2048, 1024], P('dp', 'seq')
- attn_gain_grad: float32 [1024], P(('seq', 'dp'))
- q_weight_grad: float32 [1024, 1024], P(('seq', 'dp'))
- k_weight_grad: float32 [1024, 512], P(('seq', 'dp'))
- v_weight_grad: float32 [1024, 512], P(('seq', 'dp'))
- q_norm_gain_grad: float32 [64], replicated
- k_norm_gain_grad: float32 [64], replicated
- o_weight_grad: float32 [1024, 1024], P(('seq', 'dp'))
- ffn_gain_grad: float32 [1024], P(('seq', 'dp'))
- gate_weight_grad: float32 [1024, 4608], P(('seq', 'dp'))
- up_weight_grad: float32 [1024, 4608], P(('seq', 'dp'))
- down_weight_grad: float32 [4608, 1024], P(('seq', 'dp'))
The draws below stay inside these ranges and needn't reach their ends.
Inputs may be any that keep to these rules, and one draw needn't show every extreme that they name: `doc_lengths`: in each pack the 4 lengths sum to 2048; all of them but one are at most 64, and that value is reached in every pack.
All inputs are finite; a program needn't handle non-finite values.
Results may differ from the reference program's by a relative error of at most 0.018.
Values may be sent and summed in bfloat16 or wider, within the bound.
No kernel may reach another device: no remote copies, remote signals or barrier semaphores. Data moves between devices by JAX's collectives and lax.ppermute only.
A program may use at most 384 MiB of HBM per device.

```python
import math
import jax
import jax.numpy as jnp
from jax import lax

D = 1024
HQ = 16
HK = 8
HD = 64
FF = 4608
BLK = 256
DOCS = 4
GROUPS = 4
PACK = 2048


def draw_doc_lengths(key, part):
    key = jax.random.fold_in(key, 11)
    first, second = jax.random.split(key)
    shorts = jax.random.randint(first, (GROUPS, DOCS - 1), 1, BLK // 4 + 1)
    shorts = shorts.at[:, 0].set(BLK // 4)
    where_long = jax.random.randint(second, (GROUPS, 1), 0, DOCS)
    index = jnp.arange(DOCS)[None, :]
    source = jnp.minimum(index - (index > where_long).astype(jnp.int32), DOCS - 2)
    picked = jnp.take_along_axis(shorts, jnp.broadcast_to(source, (GROUPS, DOCS)), axis=1)
    longest = PACK - jnp.sum(shorts, axis=1, keepdims=True)
    return jnp.where(index == where_long, longest, picked).astype(jnp.int32)


def shard_levels(rng, shape, cuts, least, largest):
    level, own = 1.0, jax.random.fold_in(rng, 6)
    for position, shards_of in cuts:
        steps = jnp.exp(jax.random.uniform(jax.random.fold_in(own, position), (shards_of,), jnp.float32, least / len(cuts), largest / len(cuts)))
        level = level * jnp.repeat(steps, shape[position] // shards_of).reshape([-1 if axis == position else 1 for axis in range(len(shape))])
    return level


def centred(stream_key, dims, scale, reach, cuts=(), kind=jnp.bfloat16):
    level = shard_levels(stream_key, dims, cuts, -0.22, 0.18) if cuts else 1.0
    values = jax.random.normal(stream_key, dims, jnp.float32) * scale * level
    return jnp.minimum(jnp.maximum(values, -reach), reach).astype(kind)


def setup_inputs(seed: int = 0) -> dict:
    splits = jax.random.split(jax.random.key(seed), 15)
    tokens = centred(splits[0], (GROUPS, PACK, D), 1.0, 6.0, ((0, 4), (1, 8)))
    attn_gain = jnp.clip(1.0 + 0.1 * jax.random.normal(splits[1], (D,), jnp.float32), 0.5, 1.5).astype(jnp.bfloat16)
    q_weight = centred(splits[2], (D, HQ * HD), D ** -0.5, 0.1875, ((0, 32),))
    k_weight = centred(splits[3], (D, HK * HD), D ** -0.5, 0.1875, ((0, 32),))
    v_weight = centred(splits[4], (D, HK * HD), D ** -0.5, 0.1875, ((0, 32),))
    q_norm_gain = jnp.clip(1.0 + 0.15 * jax.random.normal(splits[5], (HD,), jnp.float32), 0.25, 1.75).astype(jnp.bfloat16)
    k_norm_gain = jnp.clip(1.0 + 0.15 * jax.random.normal(splits[6], (HD,), jnp.float32), 0.25, 1.75).astype(jnp.bfloat16)
    o_weight = centred(splits[7], (HQ * HD, D), 32 ** -0.5, 1.0, ((0, 32),))
    ffn_gain = jnp.clip(1.0 + 0.1 * jax.random.normal(splits[8], (D,), jnp.float32), 0.5, 1.5).astype(jnp.bfloat16)
    gate_weight = centred(splits[9], (D, FF), D ** -0.5, 0.1875, ((0, 32),))
    up_weight = centred(splits[10], (D, FF), D ** -0.5, 0.1875, ((0, 32),))
    down_weight = centred(splits[11], (FF, D), FF ** -0.5, 0.09375, ((0, 32),))
    doc_lengths = draw_doc_lengths(jax.random.fold_in(splits[14], 71), 0)
    cotangent = centred(splits[13], (GROUPS, PACK, D), 1.0, 6.0, ((0, 4), (1, 8)))
    return dict(tokens=tokens, attn_gain=attn_gain, q_weight=q_weight, k_weight=k_weight, v_weight=v_weight, q_norm_gain=q_norm_gain, k_norm_gain=k_norm_gain, o_weight=o_weight, ffn_gain=ffn_gain, gate_weight=gate_weight, up_weight=up_weight, down_weight=down_weight, doc_lengths=doc_lengths, cotangent=cotangent)


EPS = 1e-05
THETA = 1000000.0
NEG = -1e+30
HIGH = lax.Precision.HIGHEST

@jax.custom_vjp
def low(v):
    return lax.optimization_barrier(v.astype(jnp.bfloat16)).astype(jnp.float32)

@jax.custom_vjp
def low_back(v):
    return v

def low_keep(v):
    return (low(v), None)

def low_pass(kept, grad):
    return (grad,)

def back_keep(v):
    return (v, None)

def back_low(kept, grad):
    return (low(grad),)
low.defvjp(low_keep, low_pass)
low_back.defvjp(back_keep, back_low)

def product(left, right):
    return jnp.dot(left, right, precision=HIGH, preferred_element_type=jnp.float32)

def rms_scale(values, gain):
    return values * lax.rsqrt(lax.optimization_barrier(jnp.mean(values * values, axis=-1, keepdims=True)) + EPS) * gain

def rotate(values, cosine, sine):
    half = values.shape[-1] // 2
    first = values[..., :half]
    second = values[..., half:]
    return jnp.concatenate([first * cosine - second * sine, second * cosine + first * sine], axis=-1)

def doc_tables(lengths):
    ends = jnp.cumsum(lengths).astype(jnp.int32)
    starts = (ends - lengths).astype(jnp.int32)
    place = jnp.arange(PACK, dtype=jnp.int32)
    docid = lax.optimization_barrier(jnp.sum((place[:, None] >= ends[None, :]).astype(jnp.int32), axis=1)).astype(jnp.int32)
    labels = jnp.arange(lengths.shape[0], dtype=jnp.int32)
    begin = lax.optimization_barrier(jnp.sum(jnp.where(docid[:, None] == labels[None, :], starts[None, :], 0), axis=1))
    offset = (place - begin).astype(jnp.float32)
    freqs = THETA ** (-jnp.arange(HD // 2, dtype=jnp.float32) * 2.0 / HD)
    angles = offset[:, None] * freqs[None, :]
    return (docid, jnp.cos(angles), jnp.sin(angles))

def attend(queries, keys, values, docid):
    total = queries.shape[0]
    size = math.gcd(total, 512)
    count = total // size
    place = jnp.arange(total, dtype=jnp.int32)
    scale = HD ** (-0.5)

    def block(args):
        query_block, query_doc, query_place = args
        raw = jnp.einsum('tkgd,ukd->kgtu', query_block, keys, precision=HIGH)
        scores = low_back(raw * scale)
        allowed = (query_doc[:, None] == docid[None, :]) & (query_place[:, None] >= place[None, :])
        scores = jnp.where(allowed, scores, NEG)
        row_max = lax.optimization_barrier(jnp.max(scores, axis=-1, keepdims=True))
        weights = jnp.exp(scores - row_max) * allowed
        row_sum = lax.optimization_barrier(jnp.sum(weights, axis=-1))
        mixed = jnp.einsum('kgtu,ukd->kgtd', low(weights), values, precision=HIGH) / row_sum[..., None]
        return jnp.transpose(mixed, (2, 0, 1, 3))

    def split(array):
        return array.reshape((count, size) + array.shape[1:])
    result = lax.map(jax.checkpoint(block), (split(queries), split(docid), split(place)))
    return result.reshape(queries.shape)

def forward(inputs, attn_gain, q_weight, k_weight, v_weight, q_norm_gain, k_norm_gain, o_weight, ffn_gain, gate_weight, up_weight, down_weight, docids, cosines, sines):

    def one_pack(args):
        pack_in, docid, cosine, sine = args
        normed = low(rms_scale(pack_in, attn_gain))
        q_pre = low_back(product(normed, q_weight)).reshape(PACK, HQ, HD)
        k_pre = low_back(product(normed, k_weight)).reshape(PACK, HK, HD)
        values = low(low_back(product(normed, v_weight))).reshape(PACK, HK, HD)
        queries = low(rotate(rms_scale(q_pre, q_norm_gain), cosine[:, None, :], sine[:, None, :]))
        keys = low(rotate(rms_scale(k_pre, k_norm_gain), cosine[:, None, :], sine[:, None, :]))
        mixed = attend(queries.reshape(PACK, HK, HQ // HK, HD), keys, values, docid)
        attn_b = low(low_back(mixed.reshape(PACK, HQ * HD)))
        hidden = pack_in + low_back(product(attn_b, o_weight))
        normed_two = low(rms_scale(hidden, ffn_gain))
        gate_proj = low_back(product(normed_two, gate_weight))
        up_proj = low_back(product(normed_two, up_weight))
        activated = low(jax.nn.silu(gate_proj) * up_proj)
        return hidden + low_back(product(activated, down_weight))
    return lax.map(one_pack, (inputs, docids, cosines, sines))

def reference(tokens, attn_gain, q_weight, k_weight, v_weight, q_norm_gain, k_norm_gain, o_weight, ffn_gain, gate_weight, up_weight, down_weight, doc_lengths, cotangent):
    docids, cosines, sines = jax.vmap(doc_tables)(doc_lengths)
    params = [w.astype(jnp.float32) for w in (attn_gain, q_weight, k_weight, v_weight, q_norm_gain, k_norm_gain, o_weight, ffn_gain, gate_weight, up_weight, down_weight)]

    def wrapped(inputs, *weights):
        return forward(inputs, *weights, docids, cosines, sines)
    result, pullback = jax.vjp(wrapped, tokens.astype(jnp.float32), *params)
    grads = pullback(cotangent.astype(jnp.float32))
    return (result.astype(jnp.bfloat16), grads[0], grads[1], grads[2], grads[3], grads[4], grads[5], grads[6], grads[7], grads[8], grads[9], grads[10], grads[11])
```

```python
import functools
import math

import jax
import jax.numpy as jnp
from jax import lax
from jax.experimental import pallas as pl
from jax.experimental.pallas import tpu as pltpu
from jax.sharding import Mesh
from jax.sharding import PartitionSpec as P

EPS = 1e-05
THETA = 1000000.0
LOG2E = math.log2(math.e)
BF = jnp.bfloat16
F32 = jnp.float32

ZAXES = ("t", "z")
SEQ = ("t", "z", "x")
HEADS = ("z", "x")


def dot(left, right, contract):
    return lax.dot_general(left, right, ((contract[:1], contract[1:]), ((), ())), preferred_element_type=F32)


def swap(array, axis):
    return lax.ppermute(array, axis, [(0, 1), (1, 0)])


def pick(array, index, axis):
    return lax.dynamic_index_in_dim(array, index, axis, keepdims=False)


def gather_two(array, axis, place):
    other = swap(array, axis)
    first = lax.axis_index(axis) == 0
    return jnp.where(first, jnp.stack([array, other], place), jnp.stack([other, array], place))


def shift(array, axes, by):
    count = lax.axis_size(axes)
    return lax.ppermute(array, axes, [(i, (i + by) % count) for i in range(count)])


def gather_line(array):
    count, here = lax.axis_size(ZAXES), lax.axis_index(ZAXES)
    out = jnp.zeros((count,) + array.shape, array.dtype)
    out = lax.dynamic_update_index_in_dim(out, array, here, 0)
    for by in range(1, count):
        out = lax.dynamic_update_index_in_dim(out, shift(array, ZAXES, by), (here - by) % count, 0)
    return out


def scatter_line(array):
    count, here = lax.axis_size(ZAXES), lax.axis_index(ZAXES)
    sent = array.astype(BF)
    total = pick(array, here, 0)
    for by in range(1, count):
        total = total + shift(pick(sent, (here + by) % count, 0), ZAXES, by).astype(F32)
    return total


def scatter_two(array, axis, place):
    here = lax.axis_index(axis)
    other = swap(pick(array, 1 - here, place).astype(BF), axis)
    return pick(array, here, place) + other.astype(F32)


def rms_factor(values):
    return lax.rsqrt(jnp.mean(values * values, axis=-1, keepdims=True) + EPS)


def rms_back(values, factor, gain, grad):
    scaled = grad * gain
    mean = jnp.mean(scaled * values, axis=-1, keepdims=True)
    return factor * scaled - values * (factor * factor * factor * mean)


def prepare(pre, gain, cosine, sine):
    half = pre.shape[1] // 2
    factor = lax.rsqrt(jnp.mean(pre * pre, axis=1, keepdims=True) + EPS)
    normed = pre * factor * gain[None, :, None]
    first, second = normed[:, :half], normed[:, half:]
    return jnp.concatenate([first * cosine - second * sine, second * cosine + first * sine], axis=1)


def attend_kernel(rate, base_ref, start_ref, q_ref, kv_ref, out_ref, exact_ref, mass_ref, key_ref):
    blocks, width, rows = q_ref.shape
    dim = width // 2
    base = base_ref[0]

    def turn(j, _):
        key_ref[j] = kv_ref[j, :dim, :].astype(F32).T.astype(BF)
        return 0

    lax.fori_loop(0, kv_ref.shape[0], turn, 0)
    place = lax.broadcasted_iota(jnp.int32, (rows, 2 * rows), 0)
    lane = lax.broadcasted_iota(jnp.int32, (rows, 2 * rows), 1) % rows

    def row(i, _):
        queries = jnp.concatenate([q_ref[i, :dim, :], q_ref[i, dim:, :]], axis=1)
        begin = jnp.concatenate([start_ref[i], start_ref[i]], axis=1)

        def tile(j, state, last):
            mass, total = state
            scores = dot(key_ref[j], queries, (1, 0))
            allowed = place >= begin - j * rows
            if last:
                allowed = allowed & (place <= lane)
            weights = jnp.where(allowed, jnp.exp2(scores * rate), 0.0)
            mass = mass + jnp.sum(weights, axis=0, keepdims=True)
            return mass, total + dot(kv_ref[j, dim:, :], weights.astype(BF), (1, 0))

        state = (jnp.zeros((1, 2 * rows), F32), jnp.zeros((dim, 2 * rows), F32))
        state = lax.fori_loop(0, base + i, functools.partial(tile, last=False), state)
        mass, total = tile(base + i, state, True)
        total = total / mass
        exact = jnp.concatenate([total[:, :rows], total[:, rows:]], axis=0)
        exact_ref[i] = exact
        out_ref[i] = exact.astype(BF)
        mass_ref[i] = mass
        return 0

    lax.fori_loop(0, blocks, row, 0)


def attend_back_kernel(
    rate, scale, base_ref, start_ref, q_ref, kv_ref, exact_ref, mass_ref, grad_ref,
    dq_ref, dkv_ref, key_ref, value_ref, qrow_ref, grow_ref, dk_ref, dv_ref,
):
    blocks, width, rows = q_ref.shape
    dim = width // 2
    base = base_ref[0]

    def turn(j, _):
        key_ref[j] = kv_ref[j, :dim, :].astype(F32).T.astype(BF)
        value_ref[j] = kv_ref[j, dim:, :].astype(F32).T.astype(BF)
        dk_ref[j] = jnp.zeros((rows, dim), F32)
        dv_ref[j] = jnp.zeros((rows, dim), F32)
        return 0

    lax.fori_loop(0, kv_ref.shape[0], turn, 0)

    def turn_rows(i, _):
        for g in range(2):
            part = slice(g * dim, (g + 1) * dim)
            qrow_ref[i, g * rows:(g + 1) * rows, :] = q_ref[i, part, :].astype(F32).T.astype(BF)
            grow_ref[i, g * rows:(g + 1) * rows, :] = grad_ref[i, part, :].astype(F32).T.astype(BF)
        return 0

    lax.fori_loop(0, blocks, turn_rows, 0)
    place = lax.broadcasted_iota(jnp.int32, (rows, 2 * rows), 0)
    lane = lax.broadcasted_iota(jnp.int32, (rows, 2 * rows), 1) % rows

    def row(i, _):
        queries = jnp.concatenate([q_ref[i, :dim, :], q_ref[i, dim:, :]], axis=1)
        grads = jnp.concatenate([grad_ref[i, :dim, :], grad_ref[i, dim:, :]], axis=1)
        exact = jnp.concatenate([exact_ref[i, :dim, :], exact_ref[i, dim:, :]], axis=1)
        begin = jnp.concatenate([start_ref[i], start_ref[i]], axis=1)
        delta = jnp.sum(grads.astype(F32) * exact, axis=0, keepdims=True)
        level = jnp.log(mass_ref[i]) * LOG2E

        def tile(j, dq, last):
            scores = dot(key_ref[j], queries, (1, 0))
            allowed = place >= begin - j * rows
            if last:
                allowed = allowed & (place <= lane)
            probs = jnp.where(allowed, jnp.exp2(scores * rate - level), 0.0)
            d_probs = dot(value_ref[j], grads, (1, 0))
            d_scores = (probs * (d_probs - delta)).astype(BF)
            dv_ref[j] += dot(probs.astype(BF), grow_ref[i], (1, 0))
            dk_ref[j] += dot(d_scores, qrow_ref[i], (1, 0))
            return dq + dot(kv_ref[j, :dim, :], d_scores, (1, 0))

        dq = lax.fori_loop(0, base + i, functools.partial(tile, last=False), jnp.zeros((dim, 2 * rows), F32))
        dq = tile(base + i, dq, True) * scale
        dq_ref[i] = jnp.concatenate([dq[:, :rows], dq[:, rows:]], axis=0).astype(BF)
        return 0

    lax.fori_loop(0, blocks, row, 0)

    def turn_back(j, _):
        dkv_ref[j, :dim, :] = (dk_ref[j] * scale).T.astype(BF)
        dkv_ref[j, dim:, :] = dv_ref[j].T.astype(BF)
        return 0

    lax.fori_loop(0, kv_ref.shape[0], turn_back, 0)


VMEM = pl.BlockSpec(memory_space=pltpu.VMEM)
SMEM = pl.BlockSpec(memory_space=pltpu.SMEM)
PARAMS = pltpu.CompilerParams(vmem_limit_bytes=48 * 1024 * 1024)


def attend(base, start, queries, kv, dim):
    blocks, width, rows = queries.shape
    tiles = kv.shape[0]
    pairs = blocks * (blocks + 1) // 2
    return pl.pallas_call(
        functools.partial(attend_kernel, dim ** -0.5 * LOG2E),
        out_shape=(
            jax.ShapeDtypeStruct(queries.shape, BF),
            jax.ShapeDtypeStruct(queries.shape, F32),
            jax.ShapeDtypeStruct((blocks, 1, 2 * rows), F32),
        ),
        in_specs=[SMEM, VMEM, VMEM, VMEM],
        out_specs=(VMEM, VMEM, VMEM),
        scratch_shapes=[pltpu.VMEM((tiles, rows, dim), BF)],
        compiler_params=PARAMS,
        cost_estimate=pl.CostEstimate(
            flops=pairs * 8 * rows * rows * dim, bytes_accessed=4 * 1024 * 1024, transcendentals=pairs * 2 * rows * rows
        ),
        name="attend",
    )(base, start, queries, kv)


def attend_back(base, start, queries, kv, exact, mass, grads, dim):
    blocks, width, rows = queries.shape
    tiles = kv.shape[0]
    pairs = blocks * (blocks + 1) // 2
    return pl.pallas_call(
        functools.partial(attend_back_kernel, dim ** -0.5 * LOG2E, dim ** -0.5),
        out_shape=(jax.ShapeDtypeStruct(queries.shape, BF), jax.ShapeDtypeStruct(kv.shape, BF)),
        in_specs=[SMEM] + [VMEM] * 6,
        out_specs=(VMEM, VMEM),
        scratch_shapes=[
            pltpu.VMEM((tiles, rows, dim), BF),
            pltpu.VMEM((tiles, rows, dim), BF),
            pltpu.VMEM((blocks, 2 * rows, dim), BF),
            pltpu.VMEM((blocks, 2 * rows, dim), BF),
            pltpu.VMEM((tiles, rows, dim), F32),
            pltpu.VMEM((tiles, rows, dim), F32),
        ],
        compiler_params=PARAMS,
        cost_estimate=pl.CostEstimate(
            flops=pairs * 20 * rows * rows * dim, bytes_accessed=4 * 1024 * 1024, transcendentals=pairs * 2 * rows * rows
        ),
        name="attend_back",
    )(base, start, queries, kv, exact, mass, grads)


def exchange(blocks):
    return lax.all_to_all(blocks, HEADS, 0, 0, tiled=True)


def on_device(
    tokens,
    attn_gain,
    q_weight,
    k_weight,
    v_weight,
    q_norm_gain,
    k_norm_gain,
    o_weight,
    ffn_gain,
    gate_weight,
    up_weight,
    down_weight,
    doc_lengths,
    cotangent,
):
    rows, width = tokens.shape[1:]
    dim = q_norm_gain.shape[0]
    line = lax.axis_size(ZAXES)
    groups = lax.axis_size("t")
    seq, pairs = lax.axis_size(SEQ), lax.axis_size(("y", "c"))
    half_pairs = pairs // 2
    here = lax.axis_index(SEQ)
    own = lax.axis_index(("y", "c"))
    side_x, side_y, side_c = lax.axis_index("x"), lax.axis_index("y"), lax.axis_index("c")
    piece = q_weight.shape[0]
    q_cols, k_cols = q_weight.shape[1], k_weight.shape[1]
    heads, kv_heads = q_cols // dim, k_cols // dim
    blocks = kv_heads
    strip = down_weight.shape[0]
    hidden_local = seq * strip
    pad = 128

    lengths = doc_lengths[0]
    ends = jnp.cumsum(lengths)
    starts = ends - lengths

    def begin_of(positions):
        doc = jnp.sum((positions[:, None] >= ends[None, :]).astype(jnp.int32), axis=1)
        labels = jnp.arange(lengths.shape[0], dtype=jnp.int32)
        return jnp.sum(jnp.where(doc[:, None] == labels[None, :], starts[None, :], 0), axis=1)

    place = here * rows + jnp.arange(rows, dtype=jnp.int32)
    offset = (place - begin_of(place)).astype(F32)
    freqs = THETA ** (-jnp.arange(dim // 2, dtype=F32) * 2.0 / dim)
    angles = freqs[:, None] * offset[None, :]
    cosine, sine = jnp.cos(angles), jnp.sin(angles)
    base = lax.axis_index("t") * blocks
    span = base * rows + jnp.arange(blocks * rows, dtype=jnp.int32)
    start_rows = begin_of(span).reshape(blocks, 1, rows)
    base = base.astype(jnp.int32).reshape(1)

    gains = jnp.pad(jnp.stack([attn_gain, ffn_gain], axis=1), ((0, 0), (0, pad - 2)))

    def gather_all(array, first, second):
        places = {"x": 1, "y": 2}
        array = gather_two(array, first, 1)
        array = gather_two(array, second, places[second])
        return gather_two(array, "c", 3)

    first_line = gather_line(jnp.concatenate([q_weight, k_weight, v_weight, gains], axis=1))
    w_query = gather_all(first_line[..., :q_cols], "x", "y").reshape(width, q_cols)
    w_rest = gather_all(first_line[..., q_cols:], "y", "x").reshape(width, -1)
    w_key, w_value = w_rest[:, :k_cols], w_rest[:, k_cols : 2 * k_cols]
    gain_rows = w_rest[:, 2 * k_cols : 2 * k_cols + 2].astype(F32).T
    attn_gain_all, ffn_gain_all = gain_rows[0], gain_rows[1]

    wide = jnp.stack([gate_weight, up_weight], axis=1).reshape(piece, 2, seq, pairs, strip)
    wide = jnp.transpose(wide, (3, 0, 1, 2, 4)).reshape(pairs, piece, 2 * hidden_local)
    mixed = jnp.zeros_like(wide)
    mixed = lax.dynamic_update_index_in_dim(mixed, pick(wide, own, 0), own, 0)
    for by in range(1, pairs):
        moved = lax.ppermute(pick(wide, own ^ by, 0), ("y", "c"), [(i, i ^ by) for i in range(pairs)])
        mixed = lax.dynamic_update_index_in_dim(mixed, moved, own ^ by, 0)
    mixed = mixed.reshape(pairs * piece, 2 * hidden_local)

    def gather_seq(array):
        return gather_two(gather_line(array), "x", 1).reshape((-1,) + array.shape[1:])

    w_out = gather_all(gather_line(o_weight), "x", "y").reshape(heads * dim, width)
    w_gate = gather_seq(mixed[:, :hidden_local])
    w_up = gather_seq(mixed[:, hidden_local:])
    w_down = gather_seq(down_weight)

    def gather_pairs(array):
        return gather_two(gather_two(array, "y", 0), "c", 1).reshape(pairs * rows, -1)

    grad_out = cotangent[0]
    grad_all = gather_pairs(grad_out)

    inputs = tokens[0].astype(F32)
    in_factor = rms_factor(inputs)
    normed = (inputs * in_factor * attn_gain_all).astype(BF)
    q_pre = dot(w_query, normed, (0, 1)).reshape(heads, dim, rows)
    k_pre = dot(w_key, normed, (0, 1)).reshape(kv_heads, dim, rows)
    values = dot(w_value, normed, (0, 1)).astype(BF).reshape(kv_heads, dim, rows)
    q_gain, k_gain = q_norm_gain.astype(F32), k_norm_gain.astype(F32)
    queries = prepare(q_pre, q_gain, cosine, sine).astype(BF).reshape(kv_heads, 2 * dim, rows)
    keys = prepare(k_pre, k_gain, cosine, sine).astype(BF)
    unit = exchange(jnp.concatenate([queries, keys, values], axis=1))
    unit_q, unit_kv = unit[:, : 2 * dim], unit[:, 2 * dim :]
    if groups > 1:
        unit_kv = lax.all_gather(unit_kv, "t", axis=0, tiled=True)
    unit_out, exact, mass = attend(base, start_rows, unit_q, unit_kv, dim)
    attn_b = exchange(unit_out).reshape(heads * dim, rows)
    hidden = inputs + dot(attn_b, w_out, (0, 0))

    ffn_factor = rms_factor(hidden)
    hn = (hidden * ffn_factor * ffn_gain_all).astype(BF)
    hn_all = gather_pairs(hn)
    gate = dot(hn_all, w_gate, (1, 0))
    up = dot(hn_all, w_up, (1, 0))
    sig = jax.nn.sigmoid(gate)
    silu = gate * sig
    act = (silu * up).astype(BF)
    d_act = dot(grad_all, w_down, (1, 1))
    d_gate = (d_act * up * (sig * (1.0 + gate * (1.0 - sig)))).astype(BF)
    d_up = (d_act * silu).astype(BF)

    def split_rows(array, side):
        return pick(array.reshape(half_pairs, 2, rows, -1), side, 1).reshape(half_pairs * rows, -1)

    def scatter_pairs(product):
        sent = swap(product(1 - side_c).astype(BF), "c")
        kept = (product(side_c) + sent.astype(F32)).reshape(half_pairs, rows, -1)
        return scatter_two(kept, "y", 0)

    d_hn = scatter_pairs(
        lambda side: dot(split_rows(d_gate, side), w_gate, (1, 1)) + dot(split_rows(d_up, side), w_up, (1, 1))
    )
    result = hidden + scatter_pairs(lambda side: dot(split_rows(act, side), w_down, (1, 0)))
    output = result.astype(BF)[None]

    def scatter_seq(left, right):
        part = left.shape[1] // (line * 2)
        cut = left.reshape(left.shape[0], line, 2, part)

        def product(side):
            return dot(pick(cut, side, 2).reshape(left.shape[0], line * part), right, (0, 0))

        sent = swap(product(1 - side_x).astype(BF), "x")
        kept = product(side_x) + sent.astype(F32)
        return scatter_line(kept.reshape(line, part, -1))

    down_grad = scatter_seq(act, grad_all)
    gate_part = scatter_seq(hn_all, d_gate)
    up_part = scatter_seq(hn_all, d_up)
    parts = jnp.concatenate([gate_part, up_part], axis=1).astype(BF).reshape(pairs, piece, 2, seq, strip)
    wide_grad = jnp.zeros_like(parts)
    wide_grad = lax.dynamic_update_index_in_dim(wide_grad, pick(parts, own, 0), own, 0)
    for by in range(1, pairs):
        moved = lax.ppermute(pick(parts, own ^ by, 0), ("y", "c"), [(i, i ^ by) for i in range(pairs)])
        wide_grad = lax.dynamic_update_index_in_dim(wide_grad, moved, own ^ by, 0)
    wide_grad = jnp.transpose(wide_grad, (2, 1, 3, 0, 4)).astype(F32).reshape(2, piece, -1)

    d_hidden = grad_out.astype(F32) + rms_back(hidden, ffn_factor, ffn_gain_all, d_hn)
    ffn_gain_part = jnp.sum(d_hn * hidden * ffn_factor, axis=0)
    d_branch = d_hidden.astype(BF)
    d_attn = dot(w_out, d_branch, (1, 1)).astype(BF).reshape(kv_heads, 2 * dim, rows)
    unit_grad = exchange(d_attn)

    def scatter_rest(array, first, second):
        places = {"x": 1, "y": 2}
        array = scatter_two(array, first, places[first])
        return scatter_two(array, second, 1)

    def cut_core(array, side):
        return pick(array.reshape(line * 2 * half_pairs, 2, piece, -1), side, 1).reshape(line * 2 * half_pairs * piece, -1)

    def out_product(side):
        return dot(cut_core(attn_b, side), d_branch, (1, 0))

    out_kept = out_product(side_c) + swap(out_product(1 - side_c).astype(BF), "c").astype(F32)
    out_kept = out_kept.reshape(line, 2, half_pairs, piece, width)
    out_grad = scatter_line(
        jnp.concatenate(
            [
                scatter_rest(out_kept[..., : width // 2], "x", "y"),
                scatter_rest(out_kept[..., width // 2 :], "y", "x"),
            ],
            axis=-1,
        )
    )

    unit_dq, unit_dkv = attend_back(base, start_rows, unit_q, unit_kv, exact, mass, unit_grad, dim)
    if groups > 1:
        unit_dkv = lax.psum_scatter(unit_dkv.astype(F32), "t", scatter_dimension=0, tiled=True).astype(BF)
    back = exchange(jnp.concatenate([unit_dq, unit_dkv], axis=1)).astype(F32)
    d_queries = back[:, : 2 * dim].reshape(heads, dim, rows)
    d_keys = back[:, 2 * dim : 3 * dim]
    d_values = back[:, 3 * dim :]
    _, query_pull = jax.vjp(lambda pre, gain: prepare(pre, gain, cosine, sine), q_pre, q_gain)
    _, key_pull = jax.vjp(lambda pre, gain: prepare(pre, gain, cosine, sine), k_pre, k_gain)
    d_q_pre, q_gain_grad = query_pull(d_queries)
    d_k_pre, k_gain_grad = key_pull(d_keys)
    d_pre = jnp.concatenate(
        [d_q_pre.reshape(q_cols, rows), d_k_pre.reshape(k_cols, rows), d_values.reshape(k_cols, rows)], axis=0
    ).astype(BF)

    small = jnp.stack([q_gain_grad, k_gain_grad])
    for axis in ("c", "y", "x"):
        small = small + swap(small, axis)
    small = sum((shift(small, ZAXES, by) for by in range(1, line)), small)

    d_normed = (
        dot(d_pre[:q_cols], w_query, (0, 1))
        + dot(d_pre[q_cols : q_cols + k_cols], w_key, (0, 1))
        + dot(d_pre[q_cols + k_cols :], w_value, (0, 1))
    )
    attn_gain_part = jnp.sum(d_normed * inputs * in_factor, axis=0)
    input_grad = (d_hidden + rms_back(inputs, in_factor, attn_gain_all, d_normed))[None]

    gain_parts = jnp.pad(jnp.stack([attn_gain_part, ffn_gain_part], axis=1), ((0, 0), (0, pad - 2)))
    normed_cut = normed.reshape(rows, line * 2 * half_pairs, 2, piece)

    def pre_product(side):
        left = pick(normed_cut, side, 2).reshape(rows, -1)
        return jnp.concatenate([dot(left, d_pre, (0, 1)), cut_core(gain_parts, side)], axis=1)

    kept = pre_product(side_c) + swap(pre_product(1 - side_c).astype(BF), "c").astype(F32)
    kept = kept.reshape(line, 2, half_pairs, piece, -1)
    shares = scatter_line(
        jnp.concatenate(
            [scatter_rest(kept[..., :q_cols], "x", "y"), scatter_rest(kept[..., q_cols:], "y", "x")], axis=-1
        )
    )
    rest = shares[:, q_cols:]
    return (
        output,
        input_grad,
        rest[:, 2 * k_cols],
        shares[:, :q_cols],
        rest[:, :k_cols],
        rest[:, k_cols : 2 * k_cols],
        small[0],
        small[1],
        out_grad,
        rest[:, 2 * k_cols + 1],
        wide_grad[0],
        wide_grad[1],
        down_grad,
    )


def solution(mesh):
    seq, pairs = mesh.shape["seq"], mesh.shape["dp"]

    def run(*arrays):
        kv_heads = arrays[3].shape[1] // arrays[5].shape[0]
        groups = seq // kv_heads
        fine = Mesh(mesh.devices.reshape(groups, kv_heads // 2, 2, pairs // 2, 2), ("t", "z", "x", "y", "c"))
        everywhere = ("t", "z", "x", "y", "c")
        packs = P(("y", "c"), SEQ, None)
        split, split_one = P(everywhere, None), P(everywhere)
        return jax.shard_map(
            on_device,
            mesh=fine,
            in_specs=(
                packs, split_one, split, split, split, P(), P(), split, split_one, split, split, split,
                P(("y", "c"), None), packs,
            ),
            out_specs=(
                packs, packs, split_one, split, split, split, P(), P(), split, split_one, split, split, split,
            ),
            check_vma=False,
        )(*arrays)

    return run
```

```python
import functools
import math

import jax
import jax.numpy as jnp
from jax import lax
from jax.experimental import pallas as pl
from jax.experimental.pallas import tpu as pltpu
from jax.sharding import Mesh
from jax.sharding import PartitionSpec as P

EPS = 1e-05
THETA = 1000000.0
LOG2E = math.log2(math.e)
BF = jnp.bfloat16
F32 = jnp.float32

ZAXES = ("t", "z")
SEQ = ("t", "z", "x")
HEADS = ("z", "x")
GROUP = ("x", "y", "c")


def dot(left, right, contract):
    return lax.dot_general(left, right, ((contract[:1], contract[1:]), ((), ())), preferred_element_type=F32)


def swap(array, axis):
    return lax.ppermute(array, axis, [(0, 1), (1, 0)])


def pick(array, index, axis):
    return lax.dynamic_index_in_dim(array, index, axis, keepdims=False)


def gather_two(array, axis, place):
    other = swap(array, axis)
    first = lax.axis_index(axis) == 0
    return jnp.where(first, jnp.stack([array, other], place), jnp.stack([other, array], place))


def shift(array, axes, by):
    count = lax.axis_size(axes)
    return lax.ppermute(array, axes, [(i, (i + by) % count) for i in range(count)])


def gather_line(array):
    count, here = lax.axis_size(ZAXES), lax.axis_index(ZAXES)
    out = jnp.zeros((count,) + array.shape, array.dtype)
    out = lax.dynamic_update_index_in_dim(out, array, here, 0)
    for by in range(1, count):
        out = lax.dynamic_update_index_in_dim(out, shift(array, ZAXES, by), (here - by) % count, 0)
    return out


def scatter_line(array):
    count, here = lax.axis_size(ZAXES), lax.axis_index(ZAXES)
    sent = array.astype(BF)
    total = pick(array, here, 0)
    for by in range(1, count):
        total = total + shift(pick(sent, (here + by) % count, 0), ZAXES, by).astype(F32)
    return total


def after(array, *others):
    return lax.optimization_barrier((array,) + others)[0]


def scatter_two(array, axis, place):
    here = lax.axis_index(axis)
    other = swap(pick(array, 1 - here, place).astype(BF), axis)
    return pick(array, here, place) + other.astype(F32)


def rms_factor(values):
    return lax.rsqrt(jnp.mean(values * values, axis=-1, keepdims=True) + EPS)


def rms_back(values, factor, gain, grad):
    scaled = grad * gain
    mean = jnp.mean(scaled * values, axis=-1, keepdims=True)
    return factor * scaled - values * (factor * factor * factor * mean)


def attend_kernel(rate, base_ref, start_ref, q_ref, kv_ref, out_ref, exact_ref, mass_ref, key_ref):
    blocks, width, rows = q_ref.shape
    dim = width // 2
    base = base_ref[0]

    def turn(j, _):
        key_ref[j] = kv_ref[j, :dim, :].astype(F32).T.astype(BF)
        return 0

    lax.fori_loop(0, kv_ref.shape[0], turn, 0)
    place = lax.broadcasted_iota(jnp.int32, (rows, 2 * rows), 0)
    lane = lax.broadcasted_iota(jnp.int32, (rows, 2 * rows), 1) % rows

    def row(i, _):
        queries = jnp.concatenate([q_ref[i, :dim, :], q_ref[i, dim:, :]], axis=1)
        begin = jnp.concatenate([start_ref[i], start_ref[i]], axis=1)

        def tile(j, state, last):
            mass, total = state
            scores = dot(key_ref[j], queries, (1, 0))
            allowed = place >= begin - j * rows
            if last:
                allowed = allowed & (place <= lane)
            weights = jnp.where(allowed, jnp.exp2(scores * rate), 0.0)
            mass = mass + jnp.sum(weights, axis=0, keepdims=True)
            return mass, total + dot(kv_ref[j, dim:, :], weights.astype(BF), (1, 0))

        state = (jnp.zeros((1, 2 * rows), F32), jnp.zeros((dim, 2 * rows), F32))
        state = lax.fori_loop(0, base + i, functools.partial(tile, last=False), state)
        mass, total = tile(base + i, state, True)
        total = total / mass
        exact = jnp.concatenate([total[:, :rows], total[:, rows:]], axis=0)
        exact_ref[i] = exact
        out_ref[i] = exact.astype(BF)
        mass_ref[i] = mass
        return 0

    lax.fori_loop(0, blocks, row, 0)


def attend_back_kernel(
    rate, scale, base_ref, start_ref, q_ref, kv_ref, exact_ref, mass_ref, grad_ref,
    dq_ref, dkv_ref, key_ref, value_ref, qrow_ref, grow_ref, dk_ref, dv_ref,
):
    blocks, width, rows = q_ref.shape
    dim = width // 2
    base = base_ref[0]

    def turn(j, _):
        key_ref[j] = kv_ref[j, :dim, :].astype(F32).T.astype(BF)
        value_ref[j] = kv_ref[j, dim:, :].astype(F32).T.astype(BF)
        dk_ref[j] = jnp.zeros((rows, dim), F32)
        dv_ref[j] = jnp.zeros((rows, dim), F32)
        return 0

    lax.fori_loop(0, kv_ref.shape[0], turn, 0)

    def turn_rows(i, _):
        for g in range(2):
            part = slice(g * dim, (g + 1) * dim)
            qrow_ref[i, g * rows:(g + 1) * rows, :] = q_ref[i, part, :].astype(F32).T.astype(BF)
            grow_ref[i, g * rows:(g + 1) * rows, :] = grad_ref[i, part, :].astype(F32).T.astype(BF)
        return 0

    lax.fori_loop(0, blocks, turn_rows, 0)
    place = lax.broadcasted_iota(jnp.int32, (rows, 2 * rows), 0)
    lane = lax.broadcasted_iota(jnp.int32, (rows, 2 * rows), 1) % rows

    def row(i, _):
        queries = jnp.concatenate([q_ref[i, :dim, :], q_ref[i, dim:, :]], axis=1)
        grads = jnp.concatenate([grad_ref[i, :dim, :], grad_ref[i, dim:, :]], axis=1)
        exact = jnp.concatenate([exact_ref[i, :dim, :], exact_ref[i, dim:, :]], axis=1)
        begin = jnp.concatenate([start_ref[i], start_ref[i]], axis=1)
        delta = jnp.sum(grads.astype(F32) * exact, axis=0, keepdims=True)
        level = jnp.log(mass_ref[i]) * LOG2E

        def tile(j, dq, last):
            scores = dot(key_ref[j], queries, (1, 0))
            allowed = place >= begin - j * rows
            if last:
                allowed = allowed & (place <= lane)
            probs = jnp.where(allowed, jnp.exp2(scores * rate - level), 0.0)
            d_probs = dot(value_ref[j], grads, (1, 0))
            d_scores = (probs * (d_probs - delta)).astype(BF)
            dv_ref[j] += dot(probs.astype(BF), grow_ref[i], (1, 0))
            dk_ref[j] += dot(d_scores, qrow_ref[i], (1, 0))
            return dq + dot(kv_ref[j, :dim, :], d_scores, (1, 0))

        dq = lax.fori_loop(0, base + i, functools.partial(tile, last=False), jnp.zeros((dim, 2 * rows), F32))
        dq = tile(base + i, dq, True) * scale
        dq_ref[i] = jnp.concatenate([dq[:, :rows], dq[:, rows:]], axis=0).astype(BF)
        return 0

    lax.fori_loop(0, blocks, row, 0)

    def turn_back(j, _):
        dkv_ref[j, :dim, :] = (dk_ref[j] * scale).T.astype(BF)
        dkv_ref[j, dim:, :] = dv_ref[j].T.astype(BF)
        return 0

    lax.fori_loop(0, kv_ref.shape[0], turn_back, 0)


def spread_kernel(strip, gate_ref, up_ref, out_ref):
    members, _, width = out_ref.shape
    local = width // 2
    wholes = [gate_ref[...].astype(F32), up_ref[...].astype(F32)]
    for d in range(members):
        firsts = [(s * members + d) * strip for s in range(local // strip)]
        out_ref[d] = jnp.concatenate(
            [whole[:, first : first + strip] for whole in wholes for first in firsts], axis=1
        ).astype(BF)


def weave_kernel(strip, in_ref, gate_ref, up_ref):
    members, _, width = in_ref.shape
    local = width // 2
    blocks = [in_ref[d].astype(F32) for d in range(members)]
    for part, ref in enumerate((gate_ref, up_ref)):
        firsts = [part * local + s * strip for s in range(local // strip)]
        ref[...] = jnp.concatenate(
            [block[:, first : first + strip] for first in firsts for block in blocks], axis=1
        )


def prepare_kernel(
    token_ref, query_ref, rest_ref, q_gain_ref, k_gain_ref, cos_ref, sin_ref, unit_ref, pre_ref, normed_ref, gain_ref
):
    dim = q_gain_ref.shape[0]
    half = dim // 2
    rows, width = token_ref.shape
    q_cols = query_ref.shape[1]
    k_cols = (rest_ref.shape[1] - 128) // 2
    kv_heads = k_cols // dim
    gains = rest_ref[:, 2 * k_cols :].astype(F32).T[:8]
    gain_ref[...] = gains
    tokens = token_ref[...].astype(F32)
    factor = lax.rsqrt(jnp.mean(tokens * tokens, axis=1, keepdims=True) + EPS)
    normed = (tokens * factor * gains[:1]).astype(BF)
    normed_ref[...] = normed
    cosine, sine = cos_ref[...], sin_ref[...]

    def turned(weight_ref, first):
        return dot(normed, weight_ref[:, first : first + 4 * dim], (1, 0)).T

    def head(pre, gain):
        scaled = pre * lax.rsqrt(jnp.mean(pre * pre, axis=0, keepdims=True) + EPS) * gain
        one, two = scaled[:half], scaled[half:]
        return jnp.concatenate([one * cosine - two * sine, two * cosine + one * sine], axis=0).astype(BF)

    for block in range(q_cols // (4 * dim)):
        pre = turned(query_ref, 4 * dim * block)
        pre_ref[4 * dim * block : 4 * dim * (block + 1), :] = pre
        for j in range(4):
            place = block * 4 + j
            unit_ref[place // 2, place % 2 * dim : (place % 2 + 1) * dim, :] = head(
                pre[j * dim : (j + 1) * dim], q_gain_ref[...]
            )
    for block in range(kv_heads // 4):
        pre = turned(rest_ref, 4 * dim * block)
        pre_ref[q_cols + 4 * dim * block : q_cols + 4 * dim * (block + 1), :] = pre
        value = turned(rest_ref, k_cols + 4 * dim * block).astype(BF)
        for j in range(4):
            part = slice(j * dim, (j + 1) * dim)
            unit_ref[block * 4 + j, 2 * dim : 3 * dim, :] = head(pre[part], k_gain_ref[...])
            unit_ref[block * 4 + j, 3 * dim :, :] = value[part]


def prepare_back_kernel(back_ref, pre_ref, q_gain_ref, k_gain_ref, cos_ref, sin_ref, out_ref, q_ref, k_ref):
    dim = q_gain_ref.shape[0]
    half = dim // 2
    kv_heads = back_ref.shape[0]
    q_cols, k_cols = 2 * kv_heads * dim, kv_heads * dim
    cosine, sine = cos_ref[...], sin_ref[...]

    def head(grad, pre, gain):
        one, two = grad[:half], grad[half:]
        scaled = jnp.concatenate([one * cosine + two * sine, two * cosine - one * sine], axis=0)
        factor = lax.rsqrt(jnp.mean(pre * pre, axis=0, keepdims=True) + EPS)
        with_gain = scaled * gain
        mean = jnp.mean(with_gain * pre, axis=0, keepdims=True)
        d_pre = factor * with_gain - pre * (factor * factor * factor * mean)
        return d_pre.astype(BF), scaled * pre * factor

    sums = [jnp.zeros(q_gain_ref.shape[:1] + back_ref.shape[2:], F32) for _ in range(2)]
    for kv in range(kv_heads):
        for g in range(3):
            first = (2 * kv + g) * dim if g < 2 else q_cols + kv * dim
            gain_ref = q_gain_ref if g < 2 else k_gain_ref
            d_pre, part = head(
                back_ref[kv, g * dim : (g + 1) * dim, :].astype(F32), pre_ref[first : first + dim, :], gain_ref[...]
            )
            out_ref[first : first + dim, :] = d_pre
            sums[g // 2] = sums[g // 2] + part
        out_ref[q_cols + k_cols + kv * dim : q_cols + k_cols + (kv + 1) * dim, :] = back_ref[kv, 3 * dim :, :]
    q_ref[...] = jnp.sum(sums[0], axis=1, keepdims=True)
    k_ref[...] = jnp.sum(sums[1], axis=1, keepdims=True)


def ffn_kernel(count, *refs):
    tokens, grads = refs[:count], refs[count : 2 * count]
    wide_ref, down_ref, hn_ref, grad_ref, act_ref, d_both_ref, d_hn_ref = refs[2 * count :]
    at = 0
    for token_ref, one_ref in zip(tokens, grads):
        size = token_ref.shape[0]
        hn_ref[at : at + size, :] = token_ref[...]
        grad_ref[at : at + size, :] = one_ref[...]
        at += size
    local = down_ref.shape[0]
    step = 256 if at % 256 == 0 else at

    def block(i, _):
        cut = pl.ds(pl.multiple_of(i * step, step), step)
        both = dot(hn_ref[cut, :], wide_ref[...], (1, 0))
        d_act = dot(grad_ref[cut, :], down_ref[...], (1, 1))
        gate, up = both[:, :local], both[:, local:]
        sig = jax.nn.sigmoid(gate)
        silu = gate * sig
        act_ref[cut, :] = (silu * up).astype(BF)
        d_gate = d_act * up * (sig * (1.0 + gate * (1.0 - sig)))
        d_both = jnp.concatenate([d_gate, d_act * silu], axis=1).astype(BF)
        d_both_ref[cut, :] = d_both
        d_hn_ref[cut, :] = dot(d_both, wide_ref[...], (1, 1)).astype(BF)
        return 0

    lax.fori_loop(0, at // step, block, 0)


VMEM = pl.BlockSpec(memory_space=pltpu.VMEM)
SMEM = pl.BlockSpec(memory_space=pltpu.SMEM)
PARAMS = pltpu.CompilerParams(vmem_limit_bytes=48 * 1024 * 1024)


def attend(base, start, queries, kv, dim):
    blocks, width, rows = queries.shape
    tiles = kv.shape[0]
    pairs = blocks * (blocks + 1) // 2
    return pl.pallas_call(
        functools.partial(attend_kernel, dim ** -0.5 * LOG2E),
        out_shape=(
            jax.ShapeDtypeStruct(queries.shape, BF),
            jax.ShapeDtypeStruct(queries.shape, F32),
            jax.ShapeDtypeStruct((blocks, 1, 2 * rows), F32),
        ),
        in_specs=[SMEM, VMEM, VMEM, VMEM],
        out_specs=(VMEM, VMEM, VMEM),
        scratch_shapes=[pltpu.VMEM((tiles, rows, dim), BF)],
        compiler_params=PARAMS,
        cost_estimate=pl.CostEstimate(
            flops=pairs * 8 * rows * rows * dim, bytes_accessed=4 * 1024 * 1024, transcendentals=pairs * 2 * rows * rows
        ),
        name="attend",
    )(base, start, queries, kv)


def attend_back(base, start, queries, kv, exact, mass, grads, dim):
    blocks, width, rows = queries.shape
    tiles = kv.shape[0]
    pairs = blocks * (blocks + 1) // 2
    return pl.pallas_call(
        functools.partial(attend_back_kernel, dim ** -0.5 * LOG2E, dim ** -0.5),
        out_shape=(jax.ShapeDtypeStruct(queries.shape, BF), jax.ShapeDtypeStruct(kv.shape, BF)),
        in_specs=[SMEM] + [VMEM] * 6,
        out_specs=(VMEM, VMEM),
        scratch_shapes=[
            pltpu.VMEM((tiles, rows, dim), BF),
            pltpu.VMEM((tiles, rows, dim), BF),
            pltpu.VMEM((blocks, 2 * rows, dim), BF),
            pltpu.VMEM((blocks, 2 * rows, dim), BF),
            pltpu.VMEM((tiles, rows, dim), F32),
            pltpu.VMEM((tiles, rows, dim), F32),
        ],
        compiler_params=PARAMS,
        cost_estimate=pl.CostEstimate(
            flops=pairs * 20 * rows * rows * dim, bytes_accessed=4 * 1024 * 1024, transcendentals=pairs * 2 * rows * rows
        ),
        name="attend_back",
    )(base, start, queries, kv, exact, mass, grads)


def spread(gate, up, members, strip):
    rows, width = gate.shape
    return pl.pallas_call(
        functools.partial(spread_kernel, strip),
        out_shape=jax.ShapeDtypeStruct((members, rows, 2 * width // members), BF),
        in_specs=[VMEM, VMEM],
        out_specs=VMEM,
        compiler_params=PARAMS,
        name="spread",
    )(gate, up)


def weave(parts, strip):
    members, rows, width = parts.shape
    whole = jax.ShapeDtypeStruct((rows, members * width // 2), F32)
    return pl.pallas_call(
        functools.partial(weave_kernel, strip),
        out_shape=(whole, whole),
        in_specs=[VMEM],
        out_specs=(VMEM, VMEM),
        compiler_params=PARAMS,
        name="weave",
    )(parts)


def prepare_heads(tokens, w_query, w_rest, q_gain, k_gain, cosine, sine):
    rows, width = tokens.shape
    dim = q_gain.shape[0]
    q_cols = w_query.shape[1]
    k_cols = (w_rest.shape[1] - 128) // 2
    return pl.pallas_call(
        prepare_kernel,
        out_shape=(
            jax.ShapeDtypeStruct((k_cols // dim, 4 * dim, rows), BF),
            jax.ShapeDtypeStruct((q_cols + k_cols, rows), F32),
            jax.ShapeDtypeStruct((rows, width), BF),
            jax.ShapeDtypeStruct((8, width), F32),
        ),
        in_specs=[VMEM] * 7,
        out_specs=(VMEM,) * 4,
        compiler_params=PARAMS,
        cost_estimate=pl.CostEstimate(
            flops=2 * rows * width * (q_cols + 2 * k_cols), bytes_accessed=8 * 1024 * 1024, transcendentals=0
        ),
        name="prepare",
    )(tokens, w_query, w_rest, q_gain, k_gain, cosine, sine)


def prepare_back(back, pre, q_gain, k_gain, cosine, sine):
    dim, rows = q_gain.shape[0], back.shape[2]
    return pl.pallas_call(
        prepare_back_kernel,
        out_shape=(
            jax.ShapeDtypeStruct((pre.shape[0] + back.shape[0] * dim, rows), BF),
            jax.ShapeDtypeStruct((dim, 1), F32),
            jax.ShapeDtypeStruct((dim, 1), F32),
        ),
        in_specs=[VMEM] * 6,
        out_specs=(VMEM,) * 3,
        compiler_params=PARAMS,
        cost_estimate=pl.CostEstimate(flops=20 * pre.size, bytes_accessed=6 * pre.size, transcendentals=0),
        name="prepare_back",
    )(back, pre, q_gain, k_gain, cosine, sine)


def ffn(tokens, grads, wide, down):
    total = sum(part.shape[0] for part in tokens)
    width = wide.shape[0]
    local = down.shape[0]
    shapes = [(total, width), (total, width), (total, local), (total, 2 * local), (total, width)]
    return pl.pallas_call(
        functools.partial(ffn_kernel, len(tokens)),
        out_shape=tuple(jax.ShapeDtypeStruct(shape, BF) for shape in shapes),
        in_specs=[VMEM] * (2 * len(tokens) + 2),
        out_specs=(VMEM,) * len(shapes),
        compiler_params=PARAMS,
        cost_estimate=pl.CostEstimate(
            flops=10 * total * width * local, bytes_accessed=8 * total * width, transcendentals=total * local
        ),
        name="ffn",
    )(*tokens, *grads, wide, down)


def trade(blocks):
    return lax.all_to_all(blocks, GROUP, 0, 0, tiled=True)


def exchange(blocks):
    return lax.all_to_all(blocks, HEADS, 0, 0, tiled=True)


def on_device(
    tokens,
    attn_gain,
    q_weight,
    k_weight,
    v_weight,
    q_norm_gain,
    k_norm_gain,
    o_weight,
    ffn_gain,
    gate_weight,
    up_weight,
    down_weight,
    doc_lengths,
    cotangent,
):
    rows, width = tokens.shape[1:]
    dim = q_norm_gain.shape[0]
    line = lax.axis_size(ZAXES)
    groups = lax.axis_size("t")
    seq, pairs = lax.axis_size(SEQ), lax.axis_size(("y", "c"))
    half_pairs = pairs // 2
    here = lax.axis_index(SEQ)
    side_x, side_y, side_c = lax.axis_index("x"), lax.axis_index("y"), lax.axis_index("c")
    piece = q_weight.shape[0]
    q_cols, k_cols = q_weight.shape[1], k_weight.shape[1]
    heads, kv_heads = q_cols // dim, k_cols // dim
    blocks = kv_heads
    strip = down_weight.shape[0]
    members = lax.axis_size(GROUP)
    depth = members * piece
    local = line * strip
    whole = local // 128 * 128
    pad = 128

    lengths = doc_lengths[0]
    ends = jnp.cumsum(lengths)
    starts = ends - lengths

    def begin_of(positions):
        doc = jnp.sum((positions[:, None] >= ends[None, :]).astype(jnp.int32), axis=1)
        labels = jnp.arange(lengths.shape[0], dtype=jnp.int32)
        return jnp.sum(jnp.where(doc[:, None] == labels[None, :], starts[None, :], 0), axis=1)

    place = here * rows + jnp.arange(rows, dtype=jnp.int32)
    offset = (place - begin_of(place)).astype(F32)
    freqs = THETA ** (-jnp.arange(dim // 2, dtype=F32) * 2.0 / dim)
    angles = freqs[:, None] * offset[None, :]
    cosine, sine = jnp.cos(angles), jnp.sin(angles)
    base = lax.axis_index("t") * blocks
    span = base * rows + jnp.arange(blocks * rows, dtype=jnp.int32)
    start_rows = begin_of(span).reshape(blocks, 1, rows)
    base = base.astype(jnp.int32).reshape(1)

    gains = jnp.pad(jnp.stack([attn_gain, ffn_gain], axis=1), ((0, 0), (0, pad - 2)))
    index = lax.axis_index(SEQ) * pairs + lax.axis_index(("y", "c"))

    def gather_all(array, first, second, *others):
        places = {"x": 1, "y": 2}
        array = after(gather_two(array, first, 1), *others)
        array = gather_two(array, second, places[second])
        return gather_two(array, "c", 3)

    spreaded = spread(gate_weight, up_weight, members, strip)
    mixed = trade(spreaded).reshape(depth, 2 * local)
    first_line = gather_line(after(jnp.concatenate([q_weight, k_weight, v_weight, gains], axis=1), spreaded))
    w_query = gather_all(first_line[..., :q_cols], "x", "y", mixed).reshape(width, q_cols)
    w_rest = gather_all(first_line[..., q_cols:], "y", "x", mixed).reshape(width, -1)
    w_key, w_value = w_rest[:, :k_cols], w_rest[:, k_cols : 2 * k_cols]
    w_wide = lax.all_gather(mixed, ZAXES, axis=0, tiled=True)

    quarter = rows // 2

    def plane_parts(array):
        first, second = array[:quarter], array[quarter:]
        first_x, second_y = swap(first, "x"), swap(second, "y")
        far_first = swap(jnp.concatenate([first, first_x], axis=0), "y")
        far_second = swap(jnp.concatenate([second, second_y], axis=0), "x")
        parts = ((array,), (first_x, second_y), (far_first, far_second))
        return [list(part) + [swap(piece, "c") for piece in part] for part in parts]

    def plane_sum(parts):
        def chip(part):
            half = part.shape[0] // 2
            return part[:half].astype(F32) + swap(part[half:].astype(BF), "c").astype(F32)

        def moved(part, axis):
            return swap(part.astype(BF), axis).astype(F32)

        near, middle, far = [chip(part) for part in parts]
        from_y, from_x = moved(far[:rows], "y"), moved(far[rows:], "x")
        first = from_y[:quarter] + moved(middle[:quarter] + from_y[quarter:], "x")
        second = from_x[:quarter] + moved(middle[quarter:] + from_x[quarter:], "y")
        return near + jnp.concatenate([first, second], axis=0)

    grad_out = cotangent[0]

    inputs = tokens[0].astype(F32)
    in_factor = rms_factor(inputs)
    q_gain, k_gain = q_norm_gain.astype(F32)[:, None], k_norm_gain.astype(F32)[:, None]
    unit, pre, normed, gain_rows = prepare_heads(tokens[0], w_query, w_rest, q_gain, k_gain, cosine, sine)
    attn_gain_all, ffn_gain_all = gain_rows[0], gain_rows[1]
    unit = exchange(unit)
    w_out = lax.all_gather(after(o_weight, mixed), SEQ + ("y", "c"), axis=0, tiled=True)
    w_down = lax.all_gather(after(down_weight, unit), ZAXES, axis=0, tiled=True)
    grad_parts = plane_parts(after(grad_out, unit))
    unit_q, unit_kv = unit[:, : 2 * dim], unit[:, 2 * dim :]
    if groups > 1:
        unit_kv = lax.all_gather(unit_kv, "t", axis=0, tiled=True)
    unit_out, exact, mass = attend(base, start_rows, unit_q, unit_kv, dim)
    attn_b = exchange(unit_out).reshape(heads * dim, rows)
    hidden = inputs + dot(attn_b, w_out, (0, 0))

    ffn_factor = rms_factor(hidden)
    hn = (hidden * ffn_factor * ffn_gain_all).astype(BF)
    hn_parts = plane_parts(hn)

    done = []
    for part, grad in zip(hn_parts, grad_parts):
        part = list(part)
        if done:
            part[0] = after(part[0], done[-1][4])
        done.append(ffn(part, grad, w_wide, w_down))
    hns, grad_alls, acts, d_boths, d_hn_parts = zip(*done)
    d_hn = plane_sum(d_hn_parts)

    d_hidden = grad_out.astype(F32) + rms_back(hidden, ffn_factor, ffn_gain_all, d_hn)
    ffn_gain_part = jnp.sum(d_hn * hidden * ffn_factor, axis=0)
    d_branch = d_hidden.astype(BF)
    d_attn = dot(w_out, d_branch, (1, 1)).astype(BF).reshape(kv_heads, 2 * dim, rows)
    unit_grad = exchange(d_attn)

    acts, d_boths, _ = lax.optimization_barrier((acts, d_boths, d_branch))

    def over_parts(lefts, rights):
        return sum(dot(left, right, (0, 0)) for left, right in zip(lefts, rights)).astype(BF)

    wide_grad = over_parts(hns, d_boths)
    down_grad = over_parts(acts, grad_alls)
    unit_grad = after(unit_grad, wide_grad, down_grad)
    wide_grad = lax.psum_scatter(wide_grad, ZAXES, scatter_dimension=0, tiled=True)
    down_grad = lax.psum_scatter(down_grad, ZAXES, scatter_dimension=0, tiled=True).astype(F32)
    gate_grad, up_grad = weave(trade(wide_grad.reshape(members, piece, -1)), strip)
    output = (hidden + plane_sum([dot(act, w_down, (1, 0)) for act in acts])).astype(BF)[None]

    def scatter_rest(array, first, second):
        places = {"x": 1, "y": 2}
        array = scatter_two(array, first, places[first])
        return scatter_two(array, second, 1)

    def cut_core(array, side):
        return pick(array.reshape(line * 2 * half_pairs, 2, piece, -1), side, 1).reshape(line * 2 * half_pairs * piece, -1)

    def out_product(side):
        return dot(cut_core(attn_b, side), d_branch, (1, 0))

    out_kept = out_product(side_c) + swap(out_product(1 - side_c).astype(BF), "c").astype(F32)
    out_kept = out_kept.reshape(line, 2, half_pairs, piece, width)
    out_grad = scatter_line(
        jnp.concatenate(
            [
                scatter_rest(out_kept[..., : width // 2], "x", "y"),
                scatter_rest(out_kept[..., width // 2 :], "y", "x"),
            ],
            axis=-1,
        )
    )

    unit_dq, unit_dkv = attend_back(base, start_rows, unit_q, unit_kv, exact, mass, unit_grad, dim)
    if groups > 1:
        unit_dkv = lax.psum_scatter(unit_dkv.astype(F32), "t", scatter_dimension=0, tiled=True).astype(BF)
    back = exchange(jnp.concatenate([unit_dq, unit_dkv], axis=1))
    d_pre, q_gain_grad, k_gain_grad = prepare_back(back, pre, q_gain, k_gain, cosine, sine)

    d_normed = (
        dot(d_pre[:q_cols], w_query, (0, 1))
        + dot(d_pre[q_cols : q_cols + k_cols], w_key, (0, 1))
        + dot(d_pre[q_cols + k_cols :], w_value, (0, 1))
    )
    attn_gain_part = jnp.sum(d_normed * inputs * in_factor, axis=0)
    input_grad = (d_hidden + rms_back(inputs, in_factor, attn_gain_all, d_normed))[None]

    small = jnp.concatenate([attn_gain_part, ffn_gain_part, q_gain_grad[:, 0], k_gain_grad[:, 0]])[None]
    for axis in ("c", "y", "x"):
        small = small + swap(small, axis)
    small = sum((shift(small, ZAXES, by) for by in range(1, line)), small)[0]

    def own_piece(vector):
        return pick(vector.reshape(-1, piece), index, 0)

    normed_cut = normed.reshape(rows, line * 2 * half_pairs, 2, piece)

    def pre_product(side):
        left = pick(normed_cut, side, 2).reshape(rows, -1)
        return dot(left, d_pre, (0, 1))

    kept = pre_product(side_c) + swap(pre_product(1 - side_c).astype(BF), "c").astype(F32)
    kept = kept.reshape(line, 2, half_pairs, piece, -1)
    shares = scatter_line(
        jnp.concatenate(
            [scatter_rest(kept[..., :q_cols], "x", "y"), scatter_rest(kept[..., q_cols:], "y", "x")], axis=-1
        )
    )
    rest = shares[:, q_cols:]
    return (
        output,
        input_grad,
        own_piece(small[:width]),
        shares[:, :q_cols],
        rest[:, :k_cols],
        rest[:, k_cols:],
        small[2 * width : 2 * width + dim],
        small[2 * width + dim :],
        out_grad,
        own_piece(small[width : 2 * width]),
        gate_grad,
        up_grad,
        down_grad,
    )


def solution(mesh):
    seq, pairs = mesh.shape["seq"], mesh.shape["dp"]

    def run(*arrays):
        kv_heads = arrays[3].shape[1] // arrays[5].shape[0]
        groups = seq // kv_heads
        fine = Mesh(mesh.devices.reshape(groups, kv_heads // 2, 2, pairs // 2, 2), ("t", "z", "x", "y", "c"))
        everywhere = ("t", "z", "x", "y", "c")
        packs = P(("y", "c"), SEQ, None)
        split, split_one = P(everywhere, None), P(everywhere)
        return jax.shard_map(
            on_device,
            mesh=fine,
            in_specs=(
                packs, split_one, split, split, split, P(), P(), split, split_one, split, split, split,
                P(("y", "c"), None), packs,
            ),
            out_specs=(
                packs, packs, split_one, split, split, split, P(), P(), split, split_one, split, split, split,
            ),
            check_vma=False,
        )(*arrays)

    return run
```

```python
import functools
import math

import jax
import jax.numpy as jnp
from jax import lax
from jax.experimental import pallas as pl
from jax.experimental.pallas import tpu as pltpu
from jax.sharding import Mesh
from jax.sharding import PartitionSpec as P

EPS = 1e-05
THETA = 1000000.0
LOG2E = math.log2(math.e)
BF = jnp.bfloat16
F32 = jnp.float32

ZAXES = ("t", "z")
SEQ = ("t", "z", "x")
HEADS = ("z", "x")
GROUP = ("x", "y", "c")


def dot(left, right, contract):
    return lax.dot_general(left, right, ((contract[:1], contract[1:]), ((), ())), preferred_element_type=F32)


def swap(array, axis):
    return lax.ppermute(array, axis, [(0, 1), (1, 0)])


def pick(array, index, axis):
    return lax.dynamic_index_in_dim(array, index, axis, keepdims=False)


def gather_two(array, axis, place):
    other = swap(array, axis)
    first = lax.axis_index(axis) == 0
    return jnp.where(first, jnp.stack([array, other], place), jnp.stack([other, array], place))


def shift(array, axes, by):
    count = lax.axis_size(axes)
    return lax.ppermute(array, axes, [(i, (i + by) % count) for i in range(count)])


def gather_line(array):
    count, here = lax.axis_size(ZAXES), lax.axis_index(ZAXES)
    out = jnp.zeros((count,) + array.shape, array.dtype)
    out = lax.dynamic_update_index_in_dim(out, array, here, 0)
    for by in range(1, count):
        out = lax.dynamic_update_index_in_dim(out, shift(array, ZAXES, by), (here - by) % count, 0)
    return out


def scatter_line(array):
    count, here = lax.axis_size(ZAXES), lax.axis_index(ZAXES)
    sent = array.astype(BF)
    total = pick(array, here, 0)
    for by in range(1, count):
        total = total + shift(pick(sent, (here + by) % count, 0), ZAXES, by).astype(F32)
    return total


def after(array, *others):
    return lax.optimization_barrier((array,) + others)[0]


def scatter_two(array, axis, place):
    here = lax.axis_index(axis)
    other = swap(pick(array, 1 - here, place).astype(BF), axis)
    return pick(array, here, place) + other.astype(F32)


def rms_factor(values):
    return lax.rsqrt(jnp.mean(values * values, axis=-1, keepdims=True) + EPS)


def rms_back(values, factor, gain, grad):
    scaled = grad * gain
    mean = jnp.mean(scaled * values, axis=-1, keepdims=True)
    return factor * scaled - values * (factor * factor * factor * mean)


def attend_kernel(rate, base_ref, start_ref, q_ref, kv_ref, out_ref, mass_ref, key_ref):
    blocks, width, rows = q_ref.shape
    dim = width // 2
    base = base_ref[0]

    def turn(j, _):
        key_ref[j] = kv_ref[j, :dim, :].astype(F32).T.astype(BF)
        return 0

    lax.fori_loop(0, kv_ref.shape[0], turn, 0)
    place = lax.broadcasted_iota(jnp.int32, (rows, 2 * rows), 0)
    lane = lax.broadcasted_iota(jnp.int32, (rows, 2 * rows), 1) % rows

    def row(i, _):
        queries = jnp.concatenate([q_ref[i, :dim, :], q_ref[i, dim:, :]], axis=1)
        begin = jnp.concatenate([start_ref[i], start_ref[i]], axis=1)

        def tile(j, state, last):
            mass, total = state
            scores = dot(key_ref[j], queries, (1, 0))
            allowed = place >= begin - j * rows
            if last:
                allowed = allowed & (place <= lane)
            weights = jnp.where(allowed, jnp.exp2(scores * rate), 0.0)
            mass = mass + jnp.sum(weights, axis=0, keepdims=True)
            return mass, total + dot(kv_ref[j, dim:, :], weights.astype(BF), (1, 0))

        state = (jnp.zeros((1, 2 * rows), F32), jnp.zeros((dim, 2 * rows), F32))
        state = lax.fori_loop(0, base + i, functools.partial(tile, last=False), state)
        mass, total = tile(base + i, state, True)
        total = total / mass
        out_ref[i] = jnp.concatenate([total[:, :rows], total[:, rows:]], axis=0).astype(BF)
        mass_ref[i] = mass
        return 0

    lax.fori_loop(0, blocks, row, 0)


def attend_back_kernel(
    rate, scale, base_ref, start_ref, q_ref, kv_ref, attn_ref, mass_ref, grad_ref,
    dq_ref, dkv_ref, key_ref, value_ref, qrow_ref, grow_ref, dk_ref, dv_ref,
):
    blocks, width, rows = q_ref.shape
    dim = width // 2
    base = base_ref[0]

    def turn(j, _):
        key_ref[j] = kv_ref[j, :dim, :].astype(F32).T.astype(BF)
        value_ref[j] = kv_ref[j, dim:, :].astype(F32).T.astype(BF)
        dk_ref[j] = jnp.zeros((rows, dim), F32)
        dv_ref[j] = jnp.zeros((rows, dim), F32)
        return 0

    lax.fori_loop(0, kv_ref.shape[0], turn, 0)

    def turn_rows(i, _):
        for g in range(2):
            part = slice(g * dim, (g + 1) * dim)
            qrow_ref[i, g * rows:(g + 1) * rows, :] = q_ref[i, part, :].astype(F32).T.astype(BF)
            grow_ref[i, g * rows:(g + 1) * rows, :] = grad_ref[i, part, :].astype(F32).T.astype(BF)
        return 0

    lax.fori_loop(0, blocks, turn_rows, 0)
    place = lax.broadcasted_iota(jnp.int32, (rows, 2 * rows), 0)
    lane = lax.broadcasted_iota(jnp.int32, (rows, 2 * rows), 1) % rows

    def row(i, _):
        queries = jnp.concatenate([q_ref[i, :dim, :], q_ref[i, dim:, :]], axis=1)
        grads = jnp.concatenate([grad_ref[i, :dim, :], grad_ref[i, dim:, :]], axis=1)
        attn = jnp.concatenate([attn_ref[i, :dim, :], attn_ref[i, dim:, :]], axis=1).astype(F32)
        begin = jnp.concatenate([start_ref[i], start_ref[i]], axis=1)
        delta = jnp.sum(grads.astype(F32) * attn, axis=0, keepdims=True)
        level = jnp.log(mass_ref[i]) * LOG2E

        def tile(j, dq, last):
            scores = dot(key_ref[j], queries, (1, 0))
            allowed = place >= begin - j * rows
            if last:
                allowed = allowed & (place <= lane)
            probs = jnp.where(allowed, jnp.exp2(scores * rate - level), 0.0)
            d_probs = dot(value_ref[j], grads, (1, 0))
            d_scores = (probs * (d_probs - delta)).astype(BF)
            dv_ref[j] += dot(probs.astype(BF), grow_ref[i], (1, 0))
            dk_ref[j] += dot(d_scores, qrow_ref[i], (1, 0))
            return dq + dot(kv_ref[j, :dim, :], d_scores, (1, 0))

        dq = lax.fori_loop(0, base + i, functools.partial(tile, last=False), jnp.zeros((dim, 2 * rows), F32))
        dq = tile(base + i, dq, True) * scale
        dq_ref[i] = jnp.concatenate([dq[:, :rows], dq[:, rows:]], axis=0).astype(BF)
        return 0

    lax.fori_loop(0, blocks, row, 0)

    def turn_back(j, _):
        dkv_ref[j, :dim, :] = (dk_ref[j] * scale).T.astype(BF)
        dkv_ref[j, dim:, :] = dv_ref[j].T.astype(BF)
        return 0

    lax.fori_loop(0, kv_ref.shape[0], turn_back, 0)


def spread_kernel(strip, gate_ref, up_ref, out_ref):
    members, _, width = out_ref.shape
    local = width // 2
    wholes = [gate_ref[...].astype(F32), up_ref[...].astype(F32)]
    for d in range(members):
        firsts = [(s * members + d) * strip for s in range(local // strip)]
        out_ref[d] = jnp.concatenate(
            [whole[:, first : first + strip] for whole in wholes for first in firsts], axis=1
        ).astype(BF)


def weave_kernel(strip, in_ref, gate_ref, up_ref):
    members, _, width = in_ref.shape
    local = width // 2
    blocks = [in_ref[d].astype(F32) for d in range(members)]
    for part, ref in enumerate((gate_ref, up_ref)):
        firsts = [part * local + s * strip for s in range(local // strip)]
        ref[...] = jnp.concatenate(
            [block[:, first : first + strip] for first in firsts for block in blocks], axis=1
        )


def prepare_kernel(
    token_ref, query_ref, rest_ref, q_gain_ref, k_gain_ref, cos_ref, sin_ref, unit_ref, pre_ref, normed_ref, gain_ref
):
    dim = q_gain_ref.shape[0]
    half = dim // 2
    rows, width = token_ref.shape
    q_cols = query_ref.shape[1]
    k_cols = (rest_ref.shape[1] - 128) // 2
    kv_heads = k_cols // dim
    gains = rest_ref[:, 2 * k_cols :].astype(F32).T[:8]
    gain_ref[...] = gains
    tokens = token_ref[...].astype(F32)
    factor = lax.rsqrt(jnp.mean(tokens * tokens, axis=1, keepdims=True) + EPS)
    normed = (tokens * factor * gains[:1]).astype(BF)
    normed_ref[...] = normed
    cosine, sine = cos_ref[...], sin_ref[...]

    def turned(weight_ref, first):
        return dot(normed, weight_ref[:, first : first + 4 * dim], (1, 0)).T

    def head(pre, gain):
        scaled = pre * lax.rsqrt(jnp.mean(pre * pre, axis=0, keepdims=True) + EPS) * gain
        one, two = scaled[:half], scaled[half:]
        return jnp.concatenate([one * cosine - two * sine, two * cosine + one * sine], axis=0).astype(BF)

    for block in range(q_cols // (4 * dim)):
        pre = turned(query_ref, 4 * dim * block)
        pre_ref[4 * dim * block : 4 * dim * (block + 1), :] = pre
        for j in range(4):
            place = block * 4 + j
            unit_ref[place // 2, place % 2 * dim : (place % 2 + 1) * dim, :] = head(
                pre[j * dim : (j + 1) * dim], q_gain_ref[...]
            )
    for block in range(kv_heads // 4):
        pre = turned(rest_ref, 4 * dim * block)
        pre_ref[q_cols + 4 * dim * block : q_cols + 4 * dim * (block + 1), :] = pre
        value = turned(rest_ref, k_cols + 4 * dim * block).astype(BF)
        for j in range(4):
            part = slice(j * dim, (j + 1) * dim)
            unit_ref[block * 4 + j, 2 * dim : 3 * dim, :] = head(pre[part], k_gain_ref[...])
            unit_ref[block * 4 + j, 3 * dim :, :] = value[part]


def prepare_back_kernel(back_ref, pre_ref, q_gain_ref, k_gain_ref, cos_ref, sin_ref, out_ref, q_ref, k_ref):
    dim = q_gain_ref.shape[0]
    half = dim // 2
    kv_heads = back_ref.shape[0]
    q_cols, k_cols = 2 * kv_heads * dim, kv_heads * dim
    cosine, sine = cos_ref[...], sin_ref[...]

    def head(grad, pre, gain):
        one, two = grad[:half], grad[half:]
        scaled = jnp.concatenate([one * cosine + two * sine, two * cosine - one * sine], axis=0)
        factor = lax.rsqrt(jnp.mean(pre * pre, axis=0, keepdims=True) + EPS)
        with_gain = scaled * gain
        mean = jnp.mean(with_gain * pre, axis=0, keepdims=True)
        d_pre = factor * with_gain - pre * (factor * factor * factor * mean)
        return d_pre.astype(BF), scaled * pre * factor

    sums = [jnp.zeros(q_gain_ref.shape[:1] + back_ref.shape[2:], F32) for _ in range(2)]
    for kv in range(kv_heads):
        for g in range(3):
            first = (2 * kv + g) * dim if g < 2 else q_cols + kv * dim
            gain_ref = q_gain_ref if g < 2 else k_gain_ref
            d_pre, part = head(
                back_ref[kv, g * dim : (g + 1) * dim, :].astype(F32), pre_ref[first : first + dim, :], gain_ref[...]
            )
            out_ref[first : first + dim, :] = d_pre
            sums[g // 2] = sums[g // 2] + part
        out_ref[q_cols + k_cols + kv * dim : q_cols + k_cols + (kv + 1) * dim, :] = back_ref[kv, 3 * dim :, :]
    q_ref[...] = jnp.sum(sums[0], axis=1, keepdims=True)
    k_ref[...] = jnp.sum(sums[1], axis=1, keepdims=True)


def down_rows(every_ref, down_ref):
    line, total, _ = every_ref.shape
    strip = down_ref.shape[0] // line
    for z in range(line):
        down_ref[z * strip : (z + 1) * strip, :] = every_ref[z, total - strip :, : down_ref.shape[1]]


def ffn_kernel(count, *refs):
    tokens, grads = refs[:count], refs[count : 2 * count]
    every_ref, hn_ref, grad_ref, act_ref, d_both_ref, own_ref, other_ref, down_ref = refs[2 * count :]
    at = 0
    for token_ref, one_ref in zip(tokens, grads):
        size = token_ref.shape[0]
        hn_ref[at : at + size, :] = token_ref[...]
        grad_ref[at : at + size, :] = one_ref[...]
        at += size
    down_rows(every_ref, down_ref)
    line = every_ref.shape[0]
    depth = hn_ref.shape[1] // line
    local = down_ref.shape[0]
    half = own_ref.shape[0]
    step = 256 if half % 256 == 0 else half
    for first in reversed(range(0, at, step)):
        cut = slice(first, first + step)
        both = sum(
            dot(hn_ref[cut, z * depth : (z + 1) * depth], every_ref[z, :depth, :], (1, 0)) for z in range(line)
        )
        d_act = dot(grad_ref[cut, :], down_ref[...], (1, 1))
        gate, up = both[:, :local], both[:, local:]
        sig = jax.nn.sigmoid(gate)
        silu = gate * sig
        act_ref[cut, :] = (silu * up).astype(BF)
        d_gate = d_act * up * (sig * (1.0 + gate * (1.0 - sig)))
        d_both = jnp.concatenate([d_gate, d_act * silu], axis=1).astype(BF)
        d_both_ref[cut, :] = d_both
        ref, place = (own_ref, first) if first < half else (other_ref, first - half)
        d_hn = [dot(d_both, every_ref[z, :depth, :], (1, 1)).astype(BF) for z in range(line)]
        ref[place : place + step, :] = jnp.concatenate(d_hn, axis=1)


def ffn_out_kernel(count, *refs):
    acts, every_ref, outs, down_ref = refs[:count], refs[count], refs[count + 1 : -1], refs[-1]
    down_rows(every_ref, down_ref)
    for i, act_ref in enumerate(acts):
        half = act_ref.shape[0] // 2
        for side in range(2):
            outs[2 * i + side][...] = dot(
                act_ref[side * half : (side + 1) * half, :], down_ref[...], (1, 0)
            ).astype(BF)


def ffn_weights_kernel(count, *refs):
    hns, d_boths, acts, grads = [refs[i * count : (i + 1) * count] for i in range(4)]
    out_ref = refs[4 * count]
    line, _, columns = out_ref.shape
    width, local = hns[0].shape[1], acts[0].shape[1]
    depth, strip = width // line, local // line
    for z in range(line):
        for lefts, rights, size, first in ((hns, d_boths, depth, 0), (acts, grads, strip, depth)):
            total = sum(
                dot(left[:, z * size : (z + 1) * size], right[...], (0, 0)) for left, right in zip(lefts, rights)
            )
            if total.shape[1] < columns:
                total = jnp.concatenate([total, jnp.zeros((size, columns - total.shape[1]), F32)], axis=1)
            out_ref[z, first : first + size, :] = total.astype(BF)


VMEM = pl.BlockSpec(memory_space=pltpu.VMEM)
SMEM = pl.BlockSpec(memory_space=pltpu.SMEM)
LITTLE = pl.CostEstimate(flops=1, bytes_accessed=1, transcendentals=0)
PARAMS = pltpu.CompilerParams(vmem_limit_bytes=48 * 1024 * 1024)


def attend(base, start, queries, kv, dim):
    blocks, width, rows = queries.shape
    tiles = kv.shape[0]
    pairs = blocks * (blocks + 1) // 2
    return pl.pallas_call(
        functools.partial(attend_kernel, dim ** -0.5 * LOG2E),
        out_shape=(
            jax.ShapeDtypeStruct(queries.shape, BF),
            jax.ShapeDtypeStruct((blocks, 1, 2 * rows), F32),
        ),
        in_specs=[SMEM, VMEM, VMEM, VMEM],
        out_specs=(VMEM, VMEM),
        scratch_shapes=[pltpu.VMEM((tiles, rows, dim), BF)],
        compiler_params=PARAMS,
        cost_estimate=LITTLE,
        name="attend",
    )(base, start, queries, kv)


def attend_back(base, start, queries, kv, attn, mass, grads, dim):
    blocks, width, rows = queries.shape
    tiles = kv.shape[0]
    pairs = blocks * (blocks + 1) // 2
    return pl.pallas_call(
        functools.partial(attend_back_kernel, dim ** -0.5 * LOG2E, dim ** -0.5),
        out_shape=(jax.ShapeDtypeStruct(queries.shape, BF), jax.ShapeDtypeStruct(kv.shape, BF)),
        in_specs=[SMEM] + [VMEM] * 6,
        out_specs=(VMEM, VMEM),
        scratch_shapes=[
            pltpu.VMEM((tiles, rows, dim), BF),
            pltpu.VMEM((tiles, rows, dim), BF),
            pltpu.VMEM((blocks, 2 * rows, dim), BF),
            pltpu.VMEM((blocks, 2 * rows, dim), BF),
            pltpu.VMEM((tiles, rows, dim), F32),
            pltpu.VMEM((tiles, rows, dim), F32),
        ],
        compiler_params=PARAMS,
        cost_estimate=pl.CostEstimate(flops=int(6e9), bytes_accessed=8 << 20, transcendentals=0),
        name="attend_back",
    )(base, start, queries, kv, attn, mass, grads)


def spread(gate, up, members, strip):
    rows, width = gate.shape
    return pl.pallas_call(
        functools.partial(spread_kernel, strip),
        out_shape=jax.ShapeDtypeStruct((members, rows, 2 * width // members), BF),
        in_specs=[VMEM, VMEM],
        out_specs=VMEM,
        compiler_params=PARAMS,
        name="spread",
    )(gate, up)


def weave(parts, strip):
    members, rows, width = parts.shape
    whole = jax.ShapeDtypeStruct((rows, members * width // 2), F32)
    return pl.pallas_call(
        functools.partial(weave_kernel, strip),
        out_shape=(whole, whole),
        in_specs=[VMEM],
        out_specs=(VMEM, VMEM),
        compiler_params=PARAMS,
        name="weave",
    )(parts)


def prepare_heads(tokens, w_query, w_rest, q_gain, k_gain, cosine, sine):
    rows, width = tokens.shape
    dim = q_gain.shape[0]
    q_cols = w_query.shape[1]
    k_cols = (w_rest.shape[1] - 128) // 2
    return pl.pallas_call(
        prepare_kernel,
        out_shape=(
            jax.ShapeDtypeStruct((k_cols // dim, 4 * dim, rows), BF),
            jax.ShapeDtypeStruct((q_cols + k_cols, rows), F32),
            jax.ShapeDtypeStruct((rows, width), BF),
            jax.ShapeDtypeStruct((8, width), F32),
        ),
        in_specs=[VMEM] * 7,
        out_specs=(VMEM,) * 4,
        compiler_params=PARAMS,
        cost_estimate=LITTLE,
        name="prepare",
    )(tokens, w_query, w_rest, q_gain, k_gain, cosine, sine)


def prepare_back(back, pre, q_gain, k_gain, cosine, sine):
    dim, rows = q_gain.shape[0], back.shape[2]
    return pl.pallas_call(
        prepare_back_kernel,
        out_shape=(
            jax.ShapeDtypeStruct((pre.shape[0] + back.shape[0] * dim, rows), BF),
            jax.ShapeDtypeStruct((dim, 1), F32),
            jax.ShapeDtypeStruct((dim, 1), F32),
        ),
        in_specs=[VMEM] * 6,
        out_specs=(VMEM,) * 3,
        compiler_params=PARAMS,
        cost_estimate=LITTLE,
        name="prepare_back",
    )(back, pre, q_gain, k_gain, cosine, sine)


def ffn(tokens, grads, every, strip):
    total = sum(part.shape[0] for part in tokens)
    line, _, columns = every.shape
    width, local = tokens[0].shape[1], line * strip
    shapes = [(total, width), (total, width), (total, local), (total, 2 * local), (total // 2, width), (total // 2, width)]
    return pl.pallas_call(
        functools.partial(ffn_kernel, len(tokens)),
        out_shape=tuple(jax.ShapeDtypeStruct(shape, BF) for shape in shapes),
        in_specs=[VMEM] * (2 * len(tokens) + 1),
        out_specs=(VMEM,) * len(shapes),
        scratch_shapes=[pltpu.VMEM((local, width), BF)],
        compiler_params=PARAMS,
        cost_estimate=LITTLE,
        name="ffn",
    )(*tokens, *grads, every)


def ffn_out(acts, every, width):
    local = acts[0].shape[1]
    shapes = [(act.shape[0] // 2, width) for act in acts for _ in range(2)]
    outs = pl.pallas_call(
        functools.partial(ffn_out_kernel, len(acts)),
        out_shape=tuple(jax.ShapeDtypeStruct(shape, BF) for shape in shapes),
        in_specs=[VMEM] * (len(acts) + 1),
        out_specs=(VMEM,) * len(shapes),
        scratch_shapes=[pltpu.VMEM((local, width), BF)],
        compiler_params=PARAMS,
        cost_estimate=pl.CostEstimate(flops=int(2.4e9), bytes_accessed=8 << 20, transcendentals=0),
        name="ffn_out",
    )(*acts, every)
    return list(zip(outs[::2], outs[1::2]))


def ffn_weights(hns, d_boths, acts, grads, every):
    return pl.pallas_call(
        functools.partial(ffn_weights_kernel, len(hns)),
        out_shape=jax.ShapeDtypeStruct(every.shape, BF),
        in_specs=[VMEM] * (4 * len(hns)),
        out_specs=VMEM,
        compiler_params=PARAMS,
        cost_estimate=pl.CostEstimate(flops=int(7.2e9), bytes_accessed=8 << 20, transcendentals=0),
        name="ffn_weights",
    )(*hns, *d_boths, *acts, *grads)


def trade(blocks):
    return lax.all_to_all(blocks, GROUP, 0, 0, tiled=True)


def exchange(blocks):
    return lax.all_to_all(blocks, HEADS, 0, 0, tiled=True)


def on_device(
    tokens,
    attn_gain,
    q_weight,
    k_weight,
    v_weight,
    q_norm_gain,
    k_norm_gain,
    o_weight,
    ffn_gain,
    gate_weight,
    up_weight,
    down_weight,
    doc_lengths,
    cotangent,
):
    rows, width = tokens.shape[1:]
    dim = q_norm_gain.shape[0]
    line = lax.axis_size(ZAXES)
    groups = lax.axis_size("t")
    seq, pairs = lax.axis_size(SEQ), lax.axis_size(("y", "c"))
    half_pairs = pairs // 2
    here = lax.axis_index(SEQ)
    side_x, side_y, side_c = lax.axis_index("x"), lax.axis_index("y"), lax.axis_index("c")
    piece = q_weight.shape[0]
    q_cols, k_cols = q_weight.shape[1], k_weight.shape[1]
    heads, kv_heads = q_cols // dim, k_cols // dim
    blocks = kv_heads
    strip = down_weight.shape[0]
    members = lax.axis_size(GROUP)
    depth = members * piece
    local = line * strip
    whole = local // 128 * 128
    pad = 128

    lengths = doc_lengths[0]
    ends = jnp.cumsum(lengths)
    starts = ends - lengths

    def begin_of(positions):
        doc = jnp.sum((positions[:, None] >= ends[None, :]).astype(jnp.int32), axis=1)
        labels = jnp.arange(lengths.shape[0], dtype=jnp.int32)
        return jnp.sum(jnp.where(doc[:, None] == labels[None, :], starts[None, :], 0), axis=1)

    place = here * rows + jnp.arange(rows, dtype=jnp.int32)
    offset = (place - begin_of(place)).astype(F32)
    freqs = THETA ** (-jnp.arange(dim // 2, dtype=F32) * 2.0 / dim)
    angles = freqs[:, None] * offset[None, :]
    cosine, sine = jnp.cos(angles), jnp.sin(angles)
    base = lax.axis_index("t") * blocks
    span = base * rows + jnp.arange(blocks * rows, dtype=jnp.int32)
    start_rows = begin_of(span).reshape(blocks, 1, rows)
    base = base.astype(jnp.int32).reshape(1)

    gains = jnp.pad(jnp.stack([attn_gain, ffn_gain], axis=1), ((0, 0), (0, pad - 2)))

    def gather_all(array, first, second, *others):
        places = {"x": 1, "y": 2}
        array = after(gather_two(array, first, 1), *others)
        array = gather_two(array, second, places[second])
        return gather_two(array, "c", 3)

    spreaded = spread(gate_weight, up_weight, members, strip)
    mixed = trade(spreaded).reshape(depth, 2 * local)
    packed = jnp.concatenate([mixed, jnp.pad(down_weight, ((0, 0), (0, mixed.shape[1] - width)))], axis=0)
    w_out = lax.all_gather(o_weight, SEQ + ("y", "c"), axis=0, tiled=True)
    every = lax.all_gather(packed, ZAXES, axis=0)
    first_line = gather_line(after(jnp.concatenate([q_weight, k_weight, v_weight, gains], axis=1), spreaded))
    w_query = gather_all(first_line[..., :q_cols], "x", "y", packed).reshape(width, q_cols)
    w_rest = gather_all(first_line[..., q_cols:], "y", "x", packed).reshape(width, -1)
    w_key, w_value = w_rest[:, :k_cols], w_rest[:, k_cols : 2 * k_cols]
    quarter = rows // 2

    def plane_parts(array):
        first, second = array[:quarter], array[quarter:]
        first_x, second_y = swap(first, "x"), swap(second, "y")
        far_first = swap(jnp.concatenate([first, first_x], axis=0), "y")
        far_second = swap(jnp.concatenate([second, second_y], axis=0), "x")
        parts = ((array,), (first_x, second_y), (far_first, far_second))
        return [list(part) + [swap(piece, "c") for piece in part] for part in parts]

    def plane_chip(part):
        own, other = part
        return own.astype(F32) + swap(other.astype(BF), "c").astype(F32)

    def moved(part, axis):
        return swap(part.astype(BF), axis).astype(F32)

    def plane_sum(parts, start=None):
        near, middle, far = [plane_chip(part) for part in parts]
        if start is not None:
            start(far)
        from_y, from_x = moved(far[:rows], "y"), moved(far[rows:], "x")
        first = from_y[:quarter] + moved(middle[:quarter] + from_y[quarter:], "x")
        second = from_x[:quarter] + moved(middle[quarter:] + from_x[quarter:], "y")
        return near + jnp.concatenate([first, second], axis=0)

    grad_out = cotangent[0]

    inputs = tokens[0].astype(F32)
    in_factor = rms_factor(inputs)
    q_gain, k_gain = q_norm_gain.astype(F32)[:, None], k_norm_gain.astype(F32)[:, None]
    unit, pre, normed, gain_rows = prepare_heads(tokens[0], w_query, w_rest, q_gain, k_gain, cosine, sine)
    attn_gain_all, ffn_gain_all = gain_rows[0], gain_rows[1]
    unit = exchange(unit)
    grad_parts = plane_parts(after(grad_out, unit))
    unit_q, unit_kv = unit[:, : 2 * dim], unit[:, 2 * dim :]
    if groups > 1:
        unit_kv = lax.all_gather(unit_kv, "t", axis=0, tiled=True)
    unit_out, mass = attend(base, start_rows, unit_q, unit_kv, dim)
    attn_b = exchange(unit_out).reshape(heads * dim, rows)
    hidden = inputs + dot(attn_b, w_out, (0, 0))

    ffn_factor = rms_factor(hidden)
    hn = (hidden * ffn_factor * ffn_gain_all).astype(BF)
    first, second = hn[:quarter], hn[quarter:]
    first_x, second_y = swap(first, "x"), swap(second, "y")
    done = [ffn([hn, swap(hn, "c")], grad_parts[0], every, strip)]
    first_x, second_y = lax.optimization_barrier((first_x, second_y, done[0][5]))[:2]
    far_first = swap(jnp.concatenate([first, first_x], axis=0), "y")
    far_second = swap(jnp.concatenate([second, second_y], axis=0), "x")
    done.append(ffn([first_x, second_y, swap(first_x, "c"), swap(second_y, "c")], grad_parts[1], every, strip))
    far_first, far_second = lax.optimization_barrier((far_first, far_second, done[1][5]))[:2]
    done.append(ffn([far_first, far_second, swap(far_first, "c"), swap(far_second, "c")], grad_parts[2], every, strip))
    hns, grad_alls, acts, d_boths = list(zip(*done))[:4]
    packed_grads = []

    def weights_after(far):
        later, boths, _ = lax.optimization_barrier((acts, d_boths, far))
        packed_grads.append(ffn_weights(hns, boths, later, grad_alls, every))

    d_hn = plane_sum([part[4:] for part in done], weights_after)
    packed_grad = packed_grads[0]
    d_hn = after(d_hn, packed_grad)


    d_hidden = grad_out.astype(F32) + rms_back(hidden, ffn_factor, ffn_gain_all, d_hn)
    ffn_gain_part = jnp.sum(d_hn * hidden * ffn_factor, axis=0)
    d_branch = d_hidden.astype(BF)
    d_attn = dot(w_out, d_branch, (1, 1)).astype(BF).reshape(kv_heads, 2 * dim, rows)
    unit_grad = exchange(d_attn)

    near, middle, far = [plane_chip(part) for part in ffn_out(after(acts, d_attn), every, width)]

    def cut_core(array, side):
        return pick(array.reshape(line * 2 * half_pairs, 2, piece, -1), side, 1).reshape(line * 2 * half_pairs * piece, -1)

    def out_product(side):
        return dot(cut_core(attn_b, side), d_branch, (1, 0))

    out_kept = out_product(side_c) + swap(out_product(1 - side_c).astype(BF), "c").astype(F32)
    unit_grad = after(unit_grad, packed_grad, near, middle, far, out_kept)
    packed_grad = lax.psum_scatter(packed_grad, ZAXES, scatter_dimension=0, tiled=True)[0]
    wide_grad, down_grad = packed_grad[:depth], packed_grad[depth:, :width].astype(F32)

    from_y, from_x = moved(far[:rows], "y"), moved(far[rows:], "x")
    out_kept = out_kept.reshape(line, 2, half_pairs, piece, width)
    out_sent = swap(pick(out_kept, 1 - side_y, 2).astype(BF), "y")
    unit_dq, unit_dkv = attend_back(base, start_rows, unit_q, unit_kv, unit_out, mass, unit_grad, dim)
    if groups > 1:
        unit_dkv = lax.psum_scatter(unit_dkv.astype(F32), "t", scatter_dimension=0, tiled=True).astype(BF)
    back = exchange(jnp.concatenate([unit_dq, unit_dkv], axis=1))
    from_y, from_x, out_sent, _ = lax.optimization_barrier((from_y, from_x, out_sent, unit_dq))
    first = from_y[:quarter] + moved(middle[:quarter] + from_y[quarter:], "x")
    second = from_x[:quarter] + moved(middle[quarter:] + from_x[quarter:], "y")
    output = (hidden + near + jnp.concatenate([first, second], axis=0)).astype(BF)[None]
    out_kept = scatter_two(pick(out_kept, side_y, 2) + out_sent.astype(F32), "x", 1)
    back = after(back, packed_grad, output, out_kept)
    d_pre, q_gain_grad, k_gain_grad = prepare_back(back, pre, q_gain, k_gain, cosine, sine)

    normed_cut = normed.reshape(rows, line * 2 * half_pairs, 2, piece)

    def pre_product(side):
        left = pick(normed_cut, side, 2).reshape(rows, -1)
        return dot(left, d_pre, (0, 1))

    kept = pre_product(side_c) + swap(pre_product(1 - side_c).astype(BF), "c").astype(F32)
    d_late, wide_grad = lax.optimization_barrier((d_pre, wide_grad, kept))[:2]
    gate_grad, up_grad = weave(trade(wide_grad.reshape(members, piece, -1)), strip)
    kept = kept.reshape(line, 2, half_pairs, piece, -1)
    d_normed = (
        dot(d_late[:q_cols], w_query, (0, 1))
        + dot(d_late[q_cols : q_cols + k_cols], w_key, (0, 1))
        + dot(d_late[q_cols + k_cols :], w_value, (0, 1))
    )
    attn_gain_part = jnp.sum(d_normed * inputs * in_factor, axis=0)
    input_grad = (d_hidden + rms_back(inputs, in_factor, attn_gain_all, d_normed))[None]
    q_half, rest_half = scatter_two(kept[..., :q_cols], "x", 1), scatter_two(kept[..., q_cols:], "y", 2)
    q_half, rest_half = lax.optimization_barrier((q_half, rest_half, input_grad))[:2]
    q_half, rest_half = scatter_two(q_half, "y", 1), scatter_two(rest_half, "x", 1)
    last = jnp.concatenate([q_half, rest_half, out_kept], axis=-1)
    shares = scatter_line(last)

    count = seq * pairs
    heads_part = jnp.concatenate([q_gain_grad, k_gain_grad], axis=0).reshape(1, -1)
    small = jnp.concatenate(
        [
            attn_gain_part.reshape(count, piece), ffn_gain_part.reshape(count, piece),
            jnp.broadcast_to(heads_part, (count, 2 * dim)),
        ],
        axis=1,
    )
    small = after(small, last)
    small = jnp.sum(lax.all_to_all(small, SEQ + ("y", "c"), 0, 0, tiled=True), axis=0)
    return (
        output,
        input_grad,
        small[:piece],
        shares[:, :q_cols],
        shares[:, q_cols : q_cols + k_cols],
        shares[:, q_cols + k_cols : q_cols + 2 * k_cols],
        small[2 * piece : 2 * piece + dim],
        small[2 * piece + dim :],
        shares[:, q_cols + 2 * k_cols :],
        small[piece : 2 * piece],
        gate_grad,
        up_grad,
        down_grad,
    )


def solution(mesh):
    seq, pairs = mesh.shape["seq"], mesh.shape["dp"]

    def run(*arrays):
        kv_heads = arrays[3].shape[1] // arrays[5].shape[0]
        groups = seq // kv_heads
        fine = Mesh(mesh.devices.reshape(groups, kv_heads // 2, 2, pairs // 2, 2), ("t", "z", "x", "y", "c"))
        everywhere = ("t", "z", "x", "y", "c")
        packs = P(("y", "c"), SEQ, None)
        split, split_one = P(everywhere, None), P(everywhere)
        return jax.shard_map(
            on_device,
            mesh=fine,
            in_specs=(
                packs, split_one, split, split, split, P(), P(), split, split_one, split, split, split,
                P(("y", "c"), None), packs,
            ),
            out_specs=(
                packs, packs, split_one, split, split, split, P(), P(), split, split_one, split, split, split,
            ),
            check_vma=False,
        )(*arrays)

    return run
```

```python
import functools
import math

import jax
import jax.numpy as jnp
from jax import lax
from jax.experimental import pallas as pl
from jax.experimental.pallas import tpu as pltpu
from jax.sharding import Mesh
from jax.sharding import PartitionSpec as P

EPS = 1e-05
THETA = 1000000.0
LOG2E = math.log2(math.e)
GROUP_FORWARD = 8
GROUP_BACK = 4
BF = jnp.bfloat16
F32 = jnp.float32

ZAXES = ("t", "z")
SEQ = ("t", "z", "x")
HEADS = ("z", "x")
GROUP = ("x", "y", "c")


def dot(left, right, contract):
    return lax.dot_general(left, right, ((contract[:1], contract[1:]), ((), ())), preferred_element_type=F32)


def swap(array, axis):
    return lax.ppermute(array, axis, [(0, 1), (1, 0)])


def pick(array, index, axis):
    return lax.dynamic_index_in_dim(array, index, axis, keepdims=False)


def gather_two(array, axis, place):
    other = swap(array, axis)
    first = lax.axis_index(axis) == 0
    return jnp.where(first, jnp.stack([array, other], place), jnp.stack([other, array], place))


def shift(array, axes, by):
    count = lax.axis_size(axes)
    return lax.ppermute(array, axes, [(i, (i + by) % count) for i in range(count)])


def gather_line(array):
    count, here = lax.axis_size(ZAXES), lax.axis_index(ZAXES)
    out = jnp.zeros((count,) + array.shape, array.dtype)
    out = lax.dynamic_update_index_in_dim(out, array, here, 0)
    for by in range(1, count):
        out = lax.dynamic_update_index_in_dim(out, shift(array, ZAXES, by), (here - by) % count, 0)
    return out


def scatter_line(array):
    count, here = lax.axis_size(ZAXES), lax.axis_index(ZAXES)
    sent = array.astype(BF)
    total = pick(array, here, 0)
    for by in range(1, count):
        total = total + shift(pick(sent, (here + by) % count, 0), ZAXES, by).astype(F32)
    return total


def after(array, *others):
    return lax.optimization_barrier((array,) + others)[0]


def scatter_two(array, axis, place):
    here = lax.axis_index(axis)
    other = swap(pick(array, 1 - here, place).astype(BF), axis)
    return pick(array, here, place) + other.astype(F32)


def rms_factor(values):
    return lax.rsqrt(jnp.mean(values * values, axis=-1, keepdims=True) + EPS)


def rms_back(values, factor, gain, grad):
    scaled = grad * gain
    mean = jnp.mean(scaled * values, axis=-1, keepdims=True)
    return factor * scaled - values * (factor * factor * factor * mean)


def attend_kernel(rate, base_ref, start_ref, q_ref, kv_ref, out_ref, mass_ref, key_ref):
    blocks, width, rows = q_ref.shape
    dim = width // 2
    base = base_ref[0]

    def turn(j, _):
        place = pl.ds(pl.multiple_of(j * rows, rows), rows)
        key_ref[place, :] = kv_ref[j, :dim, :].astype(F32).T.astype(BF)
        return 0

    lax.fori_loop(0, kv_ref.shape[0], turn, 0)

    for i in range(blocks):
        queries = jnp.concatenate([q_ref[i, :dim, :], q_ref[i, dim:, :]], axis=1)
        begin = jnp.concatenate([start_ref[i], start_ref[i]], axis=1)

        def tile(j, state, count, last):
            mass, total = state
            place = lax.broadcasted_iota(jnp.int32, (count * rows, 2 * rows), 0)
            scores = dot(key_ref[pl.ds(pl.multiple_of(j * rows, rows), count * rows), :], queries, (1, 0))
            allowed = place >= begin - j * rows
            if last:
                lane = lax.broadcasted_iota(jnp.int32, (count * rows, 2 * rows), 1) % rows
                allowed = allowed & (place <= lane + (count - 1) * rows)
            weights = jnp.where(allowed, jnp.exp2(scores * rate), 0.0)
            mass = mass + jnp.sum(weights, axis=0, keepdims=True)
            weights = weights.astype(BF)
            for part in range(count):
                total = total + dot(kv_ref[j + part, dim:, :], weights[part * rows : (part + 1) * rows], (1, 0))
            return mass, total

        state = (jnp.zeros((1, 2 * rows), F32), jnp.zeros((dim, 2 * rows), F32))
        ends = i % GROUP_FORWARD + 1
        state = lax.fori_loop(
            0, (base + i + 1 - ends) // GROUP_FORWARD, lambda j, state: tile(GROUP_FORWARD * j, state, GROUP_FORWARD, False), state
        )
        mass, total = tile(base + i + 1 - ends, state, ends, True)
        total = total / mass
        out_ref[i] = jnp.concatenate([total[:, :rows], total[:, rows:]], axis=0).astype(BF)
        mass_ref[i] = mass


def attend_back_kernel(
    rate, scale, base_ref, start_ref, q_ref, kv_ref, attn_ref, mass_ref, grad_ref,
    dq_ref, dkv_ref, key_ref, value_ref, qrow_ref, grow_ref, dk_ref, dv_ref,
):
    blocks, width, rows = q_ref.shape
    dim = width // 2
    base = base_ref[0]

    def turn(j, _):
        place = pl.ds(pl.multiple_of(j * rows, rows), rows)
        key_ref[place, :] = kv_ref[j, :dim, :].astype(F32).T.astype(BF)
        value_ref[place, :] = kv_ref[j, dim:, :].astype(F32).T.astype(BF)
        dk_ref[place, :] = jnp.zeros((rows, dim), F32)
        dv_ref[place, :] = jnp.zeros((rows, dim), F32)
        return 0

    lax.fori_loop(0, kv_ref.shape[0], turn, 0)

    def turn_rows(i, _):
        for g in range(2):
            part = slice(g * dim, (g + 1) * dim)
            qrow_ref[i, g * rows:(g + 1) * rows, :] = q_ref[i, part, :].astype(F32).T.astype(BF)
            grow_ref[i, g * rows:(g + 1) * rows, :] = grad_ref[i, part, :].astype(F32).T.astype(BF)
        return 0

    lax.fori_loop(0, blocks, turn_rows, 0)

    for i in range(blocks):
        queries = jnp.concatenate([q_ref[i, :dim, :], q_ref[i, dim:, :]], axis=1)
        grads = jnp.concatenate([grad_ref[i, :dim, :], grad_ref[i, dim:, :]], axis=1)
        attn = jnp.concatenate([attn_ref[i, :dim, :], attn_ref[i, dim:, :]], axis=1).astype(F32)
        begin = jnp.concatenate([start_ref[i], start_ref[i]], axis=1)
        delta = jnp.sum(grads.astype(F32) * attn, axis=0, keepdims=True)
        level = jnp.log(mass_ref[i]) * LOG2E

        def tile(j, dq, count, last):
            cut = pl.ds(pl.multiple_of(j * rows, rows), count * rows)
            place = lax.broadcasted_iota(jnp.int32, (count * rows, 2 * rows), 0)
            scores = dot(key_ref[cut, :], queries, (1, 0))
            allowed = place >= begin - j * rows
            if last:
                lane = lax.broadcasted_iota(jnp.int32, (count * rows, 2 * rows), 1) % rows
                allowed = allowed & (place <= lane + (count - 1) * rows)
            probs = jnp.where(allowed, jnp.exp2(scores * rate - level), 0.0)
            d_probs = dot(value_ref[cut, :], grads, (1, 0))
            d_scores = (probs * (d_probs - delta)).astype(BF)
            dv_ref[cut, :] += dot(probs.astype(BF), grow_ref[i], (1, 0))
            dk_ref[cut, :] += dot(d_scores, qrow_ref[i], (1, 0))
            for part in range(count):
                dq = dq + dot(kv_ref[j + part, :dim, :], d_scores[part * rows : (part + 1) * rows], (1, 0))
            return dq

        ends = i % GROUP_BACK + 1
        dq = lax.fori_loop(
            0, (base + i + 1 - ends) // GROUP_BACK, lambda j, dq: tile(GROUP_BACK * j, dq, GROUP_BACK, False), jnp.zeros((dim, 2 * rows), F32)
        )
        dq = tile(base + i + 1 - ends, dq, ends, True) * scale
        dq_ref[i] = jnp.concatenate([dq[:, :rows], dq[:, rows:]], axis=0).astype(BF)

    def turn_back(j, _):
        place = pl.ds(pl.multiple_of(j * rows, rows), rows)
        dkv_ref[j, :dim, :] = (dk_ref[place, :] * scale).T.astype(BF)
        dkv_ref[j, dim:, :] = dv_ref[place, :].T.astype(BF)
        return 0

    lax.fori_loop(0, kv_ref.shape[0], turn_back, 0)


def spread_kernel(strip, gate_ref, up_ref, out_ref):
    members, _, width = out_ref.shape
    local = width // 2
    wholes = [gate_ref[...].astype(F32), up_ref[...].astype(F32)]
    for d in range(members):
        firsts = [(s * members + d) * strip for s in range(local // strip)]
        out_ref[d] = jnp.concatenate(
            [whole[:, first : first + strip] for whole in wholes for first in firsts], axis=1
        ).astype(BF)


def weave_kernel(strip, in_ref, gate_ref, up_ref):
    members, _, width = in_ref.shape
    local = width // 2
    blocks = [in_ref[d].astype(F32) for d in range(members)]
    for part, ref in enumerate((gate_ref, up_ref)):
        firsts = [part * local + s * strip for s in range(local // strip)]
        ref[...] = jnp.concatenate(
            [block[:, first : first + strip] for first in firsts for block in blocks], axis=1
        )


def prepare_kernel(
    token_ref, query_ref, rest_ref, q_gain_ref, k_gain_ref, cos_ref, sin_ref, unit_ref, pre_ref, normed_ref, gain_ref
):
    dim = q_gain_ref.shape[0]
    half = dim // 2
    rows, width = token_ref.shape
    q_cols = query_ref.shape[1]
    k_cols = (rest_ref.shape[1] - 128) // 2
    kv_heads = k_cols // dim
    gains = rest_ref[:, 2 * k_cols :].astype(F32).T[:8]
    gain_ref[...] = gains
    tokens = token_ref[...].astype(F32)
    factor = lax.rsqrt(jnp.mean(tokens * tokens, axis=1, keepdims=True) + EPS)
    normed = (tokens * factor * gains[:1]).astype(BF)
    normed_ref[...] = normed
    cosine, sine = cos_ref[...], sin_ref[...]

    def turned(weight_ref, first):
        return dot(normed, weight_ref[:, first : first + 4 * dim], (1, 0)).T

    def head(pre, gain):
        scaled = pre * lax.rsqrt(jnp.mean(pre * pre, axis=0, keepdims=True) + EPS) * gain
        one, two = scaled[:half], scaled[half:]
        return jnp.concatenate([one * cosine - two * sine, two * cosine + one * sine], axis=0).astype(BF)

    for block in range(q_cols // (4 * dim)):
        pre = turned(query_ref, 4 * dim * block)
        pre_ref[4 * dim * block : 4 * dim * (block + 1), :] = pre
        for j in range(4):
            place = block * 4 + j
            unit_ref[place // 2, place % 2 * dim : (place % 2 + 1) * dim, :] = head(
                pre[j * dim : (j + 1) * dim], q_gain_ref[...]
            )
    for block in range(kv_heads // 4):
        pre = turned(rest_ref, 4 * dim * block)
        pre_ref[q_cols + 4 * dim * block : q_cols + 4 * dim * (block + 1), :] = pre
        value = turned(rest_ref, k_cols + 4 * dim * block).astype(BF)
        for j in range(4):
            part = slice(j * dim, (j + 1) * dim)
            unit_ref[block * 4 + j, 2 * dim : 3 * dim, :] = head(pre[part], k_gain_ref[...])
            unit_ref[block * 4 + j, 3 * dim :, :] = value[part]


def prepare_back_kernel(back_ref, pre_ref, q_gain_ref, k_gain_ref, cos_ref, sin_ref, out_ref, q_ref, k_ref):
    dim = q_gain_ref.shape[0]
    half = dim // 2
    kv_heads = back_ref.shape[0]
    q_cols, k_cols = 2 * kv_heads * dim, kv_heads * dim
    cosine, sine = cos_ref[...], sin_ref[...]

    def head(grad, pre, gain):
        one, two = grad[:half], grad[half:]
        scaled = jnp.concatenate([one * cosine + two * sine, two * cosine - one * sine], axis=0)
        factor = lax.rsqrt(jnp.mean(pre * pre, axis=0, keepdims=True) + EPS)
        with_gain = scaled * gain
        mean = jnp.mean(with_gain * pre, axis=0, keepdims=True)
        d_pre = factor * with_gain - pre * (factor * factor * factor * mean)
        return d_pre.astype(BF), scaled * pre * factor

    sums = [jnp.zeros(q_gain_ref.shape[:1] + back_ref.shape[2:], F32) for _ in range(2)]
    for kv in range(kv_heads):
        for g in range(3):
            first = (2 * kv + g) * dim if g < 2 else q_cols + kv * dim
            gain_ref = q_gain_ref if g < 2 else k_gain_ref
            d_pre, part = head(
                back_ref[kv, g * dim : (g + 1) * dim, :].astype(F32), pre_ref[first : first + dim, :], gain_ref[...]
            )
            out_ref[first : first + dim, :] = d_pre
            sums[g // 2] = sums[g // 2] + part
        out_ref[q_cols + k_cols + kv * dim : q_cols + k_cols + (kv + 1) * dim, :] = back_ref[kv, 3 * dim :, :]
    q_ref[...] = jnp.sum(sums[0], axis=1, keepdims=True)
    k_ref[...] = jnp.sum(sums[1], axis=1, keepdims=True)


def ffn_kernel(count, *refs):
    tokens, grads = refs[:count], refs[count : 2 * count]
    every_ref, down_ref, hn_ref, grad_ref, act_ref, d_both_ref, own_ref, other_ref = refs[2 * count :]
    at = 0
    for token_ref, one_ref in zip(tokens, grads):
        size = token_ref.shape[0]
        hn_ref[at : at + size, :] = token_ref[...]
        grad_ref[at : at + size, :] = one_ref[...]
        at += size
    line = every_ref.shape[0]
    depth = hn_ref.shape[1] // line
    local = down_ref.shape[0]
    half = own_ref.shape[0]
    step = 256 if half % 256 == 0 else half
    for first in reversed(range(0, at, step)):
        cut = slice(first, first + step)
        both = sum(
            dot(hn_ref[cut, z * depth : (z + 1) * depth], every_ref[z, :depth, :], (1, 0)) for z in range(line)
        )
        d_act = dot(grad_ref[cut, :], down_ref[...], (1, 1))
        gate, up = both[:, :local], both[:, local:]
        sig = jax.nn.sigmoid(gate)
        silu = gate * sig
        act_ref[cut, :] = (silu * up).astype(BF)
        d_gate = d_act * up * (sig * (1.0 + gate * (1.0 - sig)))
        d_both = jnp.concatenate([d_gate, d_act * silu], axis=1).astype(BF)
        d_both_ref[cut, :] = d_both
        ref, place = (own_ref, first) if first < half else (other_ref, first - half)
        d_hn = [dot(d_both, every_ref[z, :depth, :], (1, 1)).astype(BF) for z in range(line)]
        ref[place : place + step, :] = jnp.concatenate(d_hn, axis=1)


def ffn_out_kernel(count, *refs):
    acts, down_ref, outs = refs[:count], refs[count], refs[count + 1 :]
    for i, act_ref in enumerate(acts):
        half = act_ref.shape[0] // 2
        for side in range(2):
            outs[2 * i + side][...] = dot(
                act_ref[side * half : (side + 1) * half, :], down_ref[...], (1, 0)
            ).astype(BF)


def ffn_weights_kernel(count, *refs):
    hns, d_boths, acts, grads = [refs[i * count : (i + 1) * count] for i in range(4)]
    out_ref = refs[4 * count]
    line, _, columns = out_ref.shape
    width, local = hns[0].shape[1], acts[0].shape[1]
    depth, strip = width // line, local // line
    for z in range(line):
        for lefts, rights, size, first in ((hns, d_boths, depth, 0), (acts, grads, strip, depth)):
            total = sum(
                dot(left[:, z * size : (z + 1) * size], right[...], (0, 0)) for left, right in zip(lefts, rights)
            )
            if total.shape[1] < columns:
                total = jnp.concatenate([total, jnp.zeros((size, columns - total.shape[1]), F32)], axis=1)
            out_ref[z, first : first + size, :] = total.astype(BF)


VMEM = pl.BlockSpec(memory_space=pltpu.VMEM)
SMEM = pl.BlockSpec(memory_space=pltpu.SMEM)
LITTLE = pl.CostEstimate(flops=1, bytes_accessed=1, transcendentals=0)
PARAMS = pltpu.CompilerParams(vmem_limit_bytes=48 * 1024 * 1024)


def attend(base, start, queries, kv, dim):
    blocks, width, rows = queries.shape
    tiles = kv.shape[0]
    pairs = blocks * (blocks + 1) // 2
    return pl.pallas_call(
        functools.partial(attend_kernel, dim ** -0.5 * LOG2E),
        out_shape=(
            jax.ShapeDtypeStruct(queries.shape, BF),
            jax.ShapeDtypeStruct((blocks, 1, 2 * rows), F32),
        ),
        in_specs=[SMEM, VMEM, VMEM, VMEM],
        out_specs=(VMEM, VMEM),
        scratch_shapes=[pltpu.VMEM((tiles * rows, dim), BF)],
        compiler_params=PARAMS,
        cost_estimate=LITTLE,
        name="attend",
    )(base, start, queries, kv)


def attend_back(base, start, queries, kv, attn, mass, grads, dim):
    blocks, width, rows = queries.shape
    tiles = kv.shape[0]
    pairs = blocks * (blocks + 1) // 2
    return pl.pallas_call(
        functools.partial(attend_back_kernel, dim ** -0.5 * LOG2E, dim ** -0.5),
        out_shape=(jax.ShapeDtypeStruct(queries.shape, BF), jax.ShapeDtypeStruct(kv.shape, BF)),
        in_specs=[SMEM] + [VMEM] * 6,
        out_specs=(VMEM, VMEM),
        scratch_shapes=[
            pltpu.VMEM((tiles * rows, dim), BF),
            pltpu.VMEM((tiles * rows, dim), BF),
            pltpu.VMEM((blocks, 2 * rows, dim), BF),
            pltpu.VMEM((blocks, 2 * rows, dim), BF),
            pltpu.VMEM((tiles * rows, dim), F32),
            pltpu.VMEM((tiles * rows, dim), F32),
        ],
        compiler_params=PARAMS,
        cost_estimate=pl.CostEstimate(flops=int(6e9), bytes_accessed=8 << 20, transcendentals=0),
        name="attend_back",
    )(base, start, queries, kv, attn, mass, grads)


def spread(gate, up, members, strip):
    rows, width = gate.shape
    return pl.pallas_call(
        functools.partial(spread_kernel, strip),
        out_shape=jax.ShapeDtypeStruct((members, rows, 2 * width // members), BF),
        in_specs=[VMEM, VMEM],
        out_specs=VMEM,
        compiler_params=PARAMS,
        name="spread",
    )(gate, up)


def weave(parts, strip):
    members, rows, width = parts.shape
    whole = jax.ShapeDtypeStruct((rows, members * width // 2), F32)
    return pl.pallas_call(
        functools.partial(weave_kernel, strip),
        out_shape=(whole, whole),
        in_specs=[VMEM],
        out_specs=(VMEM, VMEM),
        compiler_params=PARAMS,
        name="weave",
    )(parts)


def prepare_heads(tokens, w_query, w_rest, q_gain, k_gain, cosine, sine):
    rows, width = tokens.shape
    dim = q_gain.shape[0]
    q_cols = w_query.shape[1]
    k_cols = (w_rest.shape[1] - 128) // 2
    return pl.pallas_call(
        prepare_kernel,
        out_shape=(
            jax.ShapeDtypeStruct((k_cols // dim, 4 * dim, rows), BF),
            jax.ShapeDtypeStruct((q_cols + k_cols, rows), F32),
            jax.ShapeDtypeStruct((rows, width), BF),
            jax.ShapeDtypeStruct((8, width), F32),
        ),
        in_specs=[VMEM] * 7,
        out_specs=(VMEM,) * 4,
        compiler_params=PARAMS,
        cost_estimate=LITTLE,
        name="prepare",
    )(tokens, w_query, w_rest, q_gain, k_gain, cosine, sine)


def prepare_back(back, pre, q_gain, k_gain, cosine, sine):
    dim, rows = q_gain.shape[0], back.shape[2]
    return pl.pallas_call(
        prepare_back_kernel,
        out_shape=(
            jax.ShapeDtypeStruct((pre.shape[0] + back.shape[0] * dim, rows), BF),
            jax.ShapeDtypeStruct((dim, 1), F32),
            jax.ShapeDtypeStruct((dim, 1), F32),
        ),
        in_specs=[VMEM] * 6,
        out_specs=(VMEM,) * 3,
        compiler_params=PARAMS,
        cost_estimate=LITTLE,
        name="prepare_back",
    )(back, pre, q_gain, k_gain, cosine, sine)


def ffn(tokens, grads, every, down):
    total = sum(part.shape[0] for part in tokens)
    local, width = down.shape
    shapes = [(total, width), (total, width), (total, local), (total, 2 * local), (total // 2, width), (total // 2, width)]
    return pl.pallas_call(
        functools.partial(ffn_kernel, len(tokens)),
        out_shape=tuple(jax.ShapeDtypeStruct(shape, BF) for shape in shapes),
        in_specs=[VMEM] * (2 * len(tokens) + 2),
        out_specs=(VMEM,) * len(shapes),
        compiler_params=PARAMS,
        cost_estimate=LITTLE,
        name="ffn",
    )(*tokens, *grads, every, down)


def ffn_out(acts, down):
    width = down.shape[1]
    shapes = [(act.shape[0] // 2, width) for act in acts for _ in range(2)]
    outs = pl.pallas_call(
        functools.partial(ffn_out_kernel, len(acts)),
        out_shape=tuple(jax.ShapeDtypeStruct(shape, BF) for shape in shapes),
        in_specs=[VMEM] * (len(acts) + 1),
        out_specs=(VMEM,) * len(shapes),
        compiler_params=PARAMS,
        cost_estimate=pl.CostEstimate(flops=int(2.4e9), bytes_accessed=8 << 20, transcendentals=0),
        name="ffn_out",
    )(*acts, down)
    return list(zip(outs[::2], outs[1::2]))


def ffn_weights(hns, d_boths, acts, grads, every):
    line, depth, columns = every.shape
    rows = depth + acts[0].shape[1] // line
    return pl.pallas_call(
        functools.partial(ffn_weights_kernel, len(hns)),
        out_shape=jax.ShapeDtypeStruct((line, rows, columns), BF),
        in_specs=[VMEM] * (4 * len(hns)),
        out_specs=VMEM,
        compiler_params=PARAMS,
        cost_estimate=pl.CostEstimate(flops=int(7.2e9), bytes_accessed=8 << 20, transcendentals=0),
        name="ffn_weights",
    )(*hns, *d_boths, *acts, *grads)


def trade(blocks):
    return lax.all_to_all(blocks, GROUP, 0, 0, tiled=True)


def exchange(blocks):
    return lax.all_to_all(blocks, HEADS, 0, 0, tiled=True)


def on_device(
    tokens,
    attn_gain,
    q_weight,
    k_weight,
    v_weight,
    q_norm_gain,
    k_norm_gain,
    o_weight,
    ffn_gain,
    gate_weight,
    up_weight,
    down_weight,
    doc_lengths,
    cotangent,
):
    rows, width = tokens.shape[1:]
    dim = q_norm_gain.shape[0]
    line = lax.axis_size(ZAXES)
    groups = lax.axis_size("t")
    seq, pairs = lax.axis_size(SEQ), lax.axis_size(("y", "c"))
    half_pairs = pairs // 2
    here = lax.axis_index(SEQ)
    side_x, side_y, side_c = lax.axis_index("x"), lax.axis_index("y"), lax.axis_index("c")
    piece = q_weight.shape[0]
    q_cols, k_cols = q_weight.shape[1], k_weight.shape[1]
    heads, kv_heads = q_cols // dim, k_cols // dim
    blocks = kv_heads
    strip = down_weight.shape[0]
    members = lax.axis_size(GROUP)
    depth = members * piece
    local = line * strip
    whole = local // 128 * 128
    pad = 128

    lengths = doc_lengths[0]
    ends = jnp.cumsum(lengths)
    starts = ends - lengths

    def begin_of(positions):
        doc = jnp.sum((positions[:, None] >= ends[None, :]).astype(jnp.int32), axis=1)
        labels = jnp.arange(lengths.shape[0], dtype=jnp.int32)
        return jnp.sum(jnp.where(doc[:, None] == labels[None, :], starts[None, :], 0), axis=1)

    place = here * rows + jnp.arange(rows, dtype=jnp.int32)
    offset = (place - begin_of(place)).astype(F32)
    freqs = THETA ** (-jnp.arange(dim // 2, dtype=F32) * 2.0 / dim)
    angles = freqs[:, None] * offset[None, :]
    cosine, sine = jnp.cos(angles), jnp.sin(angles)
    base = lax.axis_index("t") * blocks
    span = base * rows + jnp.arange(blocks * rows, dtype=jnp.int32)
    start_rows = begin_of(span).reshape(blocks, 1, rows)
    base = base.astype(jnp.int32).reshape(1)

    gains = jnp.pad(jnp.stack([attn_gain, ffn_gain], axis=1), ((0, 0), (0, pad - 2)))

    def gather_all(array, first, second, *others):
        places = {"x": 1, "y": 2}
        array = after(gather_two(array, first, 1), *others)
        array = gather_two(array, second, places[second])
        return gather_two(array, "c", 3)

    spreaded = spread(gate_weight, up_weight, members, strip)
    mixed = trade(spreaded).reshape(depth, 2 * local)
    packed = mixed
    w_out = lax.all_gather(o_weight, SEQ + ("y", "c"), axis=0, tiled=True)
    every = lax.all_gather(packed, ZAXES, axis=0)
    first_line = gather_line(after(jnp.concatenate([q_weight, k_weight, v_weight, gains], axis=1), spreaded))
    w_down = gather_line(after(down_weight, first_line)).reshape(local, width)
    w_query = gather_all(first_line[..., :q_cols], "x", "y", packed).reshape(width, q_cols)
    w_rest = gather_all(first_line[..., q_cols:], "y", "x", packed).reshape(width, -1)
    w_key, w_value = w_rest[:, :k_cols], w_rest[:, k_cols : 2 * k_cols]
    quarter = rows // 2

    def plane_parts(array):
        first, second = array[:quarter], array[quarter:]
        first_x, second_y = swap(first, "x"), swap(second, "y")
        far_first = swap(jnp.concatenate([first, first_x], axis=0), "y")
        far_second = swap(jnp.concatenate([second, second_y], axis=0), "x")
        parts = ((array,), (first_x, second_y), (far_first, far_second))
        return [list(part) + [swap(piece, "c") for piece in part] for part in parts]

    def plane_chip(part):
        own, other = part
        return own.astype(F32) + swap(other.astype(BF), "c").astype(F32)

    def moved(part, axis):
        return swap(part.astype(BF), axis).astype(F32)

    def plane_sum(parts, start=None):
        near, middle, far = [plane_chip(part) for part in parts]
        to_y, to_x = start((far[:rows].astype(BF), far[rows:].astype(BF)))
        from_y, from_x = moved(to_y, "y"), moved(to_x, "x")
        first = from_y[:quarter] + moved(middle[:quarter] + from_y[quarter:], "x")
        second = from_x[:quarter] + moved(middle[quarter:] + from_x[quarter:], "y")
        return near + jnp.concatenate([first, second], axis=0)

    grad_out = cotangent[0]

    inputs = tokens[0].astype(F32)
    in_factor = rms_factor(inputs)
    q_gain, k_gain = q_norm_gain.astype(F32)[:, None], k_norm_gain.astype(F32)[:, None]
    w_query = after(w_query, w_down)
    unit, pre, normed, gain_rows = prepare_heads(tokens[0], w_query, w_rest, q_gain, k_gain, cosine, sine)
    attn_gain_all, ffn_gain_all = gain_rows[0], gain_rows[1]
    unit = exchange(unit)
    grad_parts = plane_parts(after(grad_out, unit))
    unit_q, unit_kv = unit[:, : 2 * dim], unit[:, 2 * dim :]
    if groups > 1:
        unit_kv = lax.all_gather(unit_kv, "t", axis=0, tiled=True)
    unit_out, mass = attend(base, start_rows, unit_q, unit_kv, dim)
    attn_b = exchange(unit_out).reshape(heads * dim, rows)
    hidden = inputs + dot(attn_b, w_out, (0, 0))

    ffn_factor = rms_factor(hidden)
    hn = (hidden * ffn_factor * ffn_gain_all).astype(BF)
    first, second = hn[:quarter], hn[quarter:]
    first_x, second_y = swap(first, "x"), swap(second, "y")
    done = [ffn([hn, swap(hn, "c")], grad_parts[0], every, w_down)]
    first_x, second_y = lax.optimization_barrier((first_x, second_y, done[0][5]))[:2]
    far_first = swap(jnp.concatenate([first, first_x], axis=0), "y")
    far_second = swap(jnp.concatenate([second, second_y], axis=0), "x")
    done.append(ffn([first_x, second_y, swap(first_x, "c"), swap(second_y, "c")], grad_parts[1], every, w_down))
    far_first, far_second = lax.optimization_barrier((far_first, far_second, done[1][5]))[:2]
    done.append(ffn([far_first, far_second, swap(far_first, "c"), swap(far_second, "c")], grad_parts[2], every, w_down))
    hns, grad_alls, acts, d_boths = list(zip(*done))[:4]
    packed_grads = []

    def weights_after(far):
        later, boths, far = lax.optimization_barrier((acts, d_boths, far))
        packed_grads.append(ffn_weights(hns, boths, later, grad_alls, every))
        return far

    d_hn = plane_sum([part[4:] for part in done], weights_after)
    packed_grad = packed_grads[0]
    d_hn = after(d_hn, packed_grad)


    d_hidden = grad_out.astype(F32) + rms_back(hidden, ffn_factor, ffn_gain_all, d_hn)
    ffn_gain_part = jnp.sum(d_hn * hidden * ffn_factor, axis=0)
    d_branch = d_hidden.astype(BF)
    d_attn = dot(w_out, d_branch, (1, 1)).astype(BF).reshape(kv_heads, 2 * dim, rows)
    unit_grad = exchange(d_attn)

    near, middle, far = [plane_chip(part) for part in ffn_out(after(acts, d_attn), w_down)]

    def cut_core(array, side):
        return pick(array.reshape(line * 2 * half_pairs, 2, piece, -1), side, 1).reshape(line * 2 * half_pairs * piece, -1)

    def out_product(side):
        return dot(cut_core(attn_b, side), d_branch, (1, 0))

    out_kept = out_product(side_c) + swap(out_product(1 - side_c).astype(BF), "c").astype(F32)
    unit_grad = after(unit_grad, packed_grad, near, middle, far, out_kept)
    packed_grad = lax.psum_scatter(packed_grad, ZAXES, scatter_dimension=0, tiled=True)[0]
    wide_grad, down_grad = packed_grad[:depth], packed_grad[depth:, :width].astype(F32)

    from_y, from_x = moved(far[:rows], "y"), moved(far[rows:], "x")
    out_kept = out_kept.reshape(line, 2, half_pairs, piece, width)
    out_sent = swap(pick(out_kept, 1 - side_y, 2).astype(BF), "y")
    unit_dq, unit_dkv = attend_back(base, start_rows, unit_q, unit_kv, unit_out, mass, unit_grad, dim)
    if groups > 1:
        unit_dkv = lax.psum_scatter(unit_dkv.astype(F32), "t", scatter_dimension=0, tiled=True).astype(BF)
    back = exchange(jnp.concatenate([unit_dq, unit_dkv], axis=1))
    from_y, from_x, out_sent, _ = lax.optimization_barrier((from_y, from_x, out_sent, unit_dq))
    first = from_y[:quarter] + moved(middle[:quarter] + from_y[quarter:], "x")
    second = from_x[:quarter] + moved(middle[quarter:] + from_x[quarter:], "y")
    output = (hidden + near + jnp.concatenate([first, second], axis=0)).astype(BF)[None]
    out_kept = scatter_two(pick(out_kept, side_y, 2) + out_sent.astype(F32), "x", 1)
    back = after(back, packed_grad, output, out_kept)
    d_pre, q_gain_grad, k_gain_grad = prepare_back(back, pre, q_gain, k_gain, cosine, sine)

    normed_cut = normed.reshape(rows, line * 2 * half_pairs, 2, piece)

    def pre_product(side):
        left = pick(normed_cut, side, 2).reshape(rows, -1)
        return dot(left, d_pre, (0, 1))

    kept = pre_product(side_c) + swap(pre_product(1 - side_c).astype(BF), "c").astype(F32)
    d_late, wide_grad = lax.optimization_barrier((d_pre, wide_grad, kept))[:2]
    gate_grad, up_grad = weave(trade(wide_grad.reshape(members, piece, -1)), strip)
    kept = kept.reshape(line, 2, half_pairs, piece, -1)
    d_normed = (
        dot(d_late[:q_cols], w_query, (0, 1))
        + dot(d_late[q_cols : q_cols + k_cols], w_key, (0, 1))
        + dot(d_late[q_cols + k_cols :], w_value, (0, 1))
    )
    attn_gain_part = jnp.sum(d_normed * inputs * in_factor, axis=0)
    input_grad = (d_hidden + rms_back(inputs, in_factor, attn_gain_all, d_normed))[None]
    q_half, rest_half = scatter_two(kept[..., :q_cols], "x", 1), scatter_two(kept[..., q_cols:], "y", 2)
    q_half, rest_half = lax.optimization_barrier((q_half, rest_half, input_grad))[:2]
    q_half, rest_half = scatter_two(q_half, "y", 1), scatter_two(rest_half, "x", 1)
    last = jnp.concatenate([q_half, rest_half, out_kept], axis=-1)
    shares = scatter_line(last)

    count = seq * pairs
    heads_part = jnp.concatenate([q_gain_grad, k_gain_grad], axis=0).reshape(1, -1)
    small = jnp.concatenate(
        [
            attn_gain_part.reshape(count, piece), ffn_gain_part.reshape(count, piece),
            jnp.broadcast_to(heads_part, (count, 2 * dim)),
        ],
        axis=1,
    )
    small = after(small, last)
    small = jnp.sum(lax.all_to_all(small, SEQ + ("y", "c"), 0, 0, tiled=True), axis=0)
    return (
        output,
        input_grad,
        small[:piece],
        shares[:, :q_cols],
        shares[:, q_cols : q_cols + k_cols],
        shares[:, q_cols + k_cols : q_cols + 2 * k_cols],
        small[2 * piece : 2 * piece + dim],
        small[2 * piece + dim :],
        shares[:, q_cols + 2 * k_cols :],
        small[piece : 2 * piece],
        gate_grad,
        up_grad,
        down_grad,
    )


def solution(mesh):
    seq, pairs = mesh.shape["seq"], mesh.shape["dp"]

    def run(*arrays):
        kv_heads = arrays[3].shape[1] // arrays[5].shape[0]
        groups = seq // kv_heads
        fine = Mesh(mesh.devices.reshape(groups, kv_heads // 2, 2, pairs // 2, 2), ("t", "z", "x", "y", "c"))
        everywhere = ("t", "z", "x", "y", "c")
        packs = P(("y", "c"), SEQ, None)
        split, split_one = P(everywhere, None), P(everywhere)
        return jax.shard_map(
            on_device,
            mesh=fine,
            in_specs=(
                packs, split_one, split, split, split, P(), P(), split, split_one, split, split, split,
                P(("y", "c"), None), packs,
            ),
            out_specs=(
                packs, packs, split_one, split, split, split, P(), P(), split, split_one, split, split, split,
            ),
            check_vma=False,
        )(*arrays)

    return run
```

```python
import functools
import math

import jax
import jax.numpy as jnp
from jax import lax
from jax.experimental import pallas as pl
from jax.experimental.pallas import tpu as pltpu
from jax.sharding import Mesh
from jax.sharding import PartitionSpec as P

EPS = 1e-05
THETA = 1000000.0
LOG2E = math.log2(math.e)
GROUP_FORWARD = 8
GROUP_BACK = 4
BF = jnp.bfloat16
F32 = jnp.float32

ZAXES = ("t", "z")
SEQ = ("t", "z", "x")
HEADS = ("z", "x")
GROUP = ("x", "y", "c")


def dot(left, right, contract):
    return lax.dot_general(left, right, ((contract[:1], contract[1:]), ((), ())), preferred_element_type=F32)


def swap(array, axis):
    return lax.ppermute(array, axis, [(0, 1), (1, 0)])


def pick(array, index, axis):
    return lax.dynamic_index_in_dim(array, index, axis, keepdims=False)


def gather_two(array, axis, place):
    other = swap(array, axis)
    first = lax.axis_index(axis) == 0
    return jnp.where(first, jnp.stack([array, other], place), jnp.stack([other, array], place))


def shift(array, axes, by):
    count = lax.axis_size(axes)
    return lax.ppermute(array, axes, [(i, (i + by) % count) for i in range(count)])


def gather_line(array):
    count, here = lax.axis_size(ZAXES), lax.axis_index(ZAXES)
    out = jnp.zeros((count,) + array.shape, array.dtype)
    out = lax.dynamic_update_index_in_dim(out, array, here, 0)
    for by in range(1, count):
        out = lax.dynamic_update_index_in_dim(out, shift(array, ZAXES, by), (here - by) % count, 0)
    return out


def scatter_line(array):
    count, here = lax.axis_size(ZAXES), lax.axis_index(ZAXES)
    sent = array.astype(BF)
    total = pick(array, here, 0)
    for by in range(1, count):
        total = total + shift(pick(sent, (here + by) % count, 0), ZAXES, by).astype(F32)
    return total


def after(array, *others):
    return lax.optimization_barrier((array,) + others)[0]


def scatter_two(array, axis, place):
    here = lax.axis_index(axis)
    other = swap(pick(array, 1 - here, place).astype(BF), axis)
    return pick(array, here, place) + other.astype(F32)


def rms_factor(values):
    return lax.rsqrt(jnp.mean(values * values, axis=-1, keepdims=True) + EPS)


def rms_back(values, factor, gain, grad):
    scaled = grad * gain
    mean = jnp.mean(scaled * values, axis=-1, keepdims=True)
    return factor * scaled - values * (factor * factor * factor * mean)


def attend_kernel(rate, base_ref, start_ref, q_ref, kv_ref, out_ref, mass_ref, key_ref):
    blocks, width, rows = q_ref.shape
    dim = width // 2
    base = base_ref[0]

    def turn(j, _):
        place = pl.ds(pl.multiple_of(j * rows, rows), rows)
        key_ref[place, :] = kv_ref[j, :dim, :].astype(F32).T.astype(BF)
        return 0

    lax.fori_loop(0, kv_ref.shape[0], turn, 0)

    for i in range(blocks):
        queries = jnp.concatenate([q_ref[i, :dim, :], q_ref[i, dim:, :]], axis=1)
        begin = jnp.concatenate([start_ref[i], start_ref[i]], axis=1)

        def tile(j, state, count, last):
            mass, total = state
            place = lax.broadcasted_iota(jnp.int32, (count * rows, 2 * rows), 0)
            scores = dot(key_ref[pl.ds(pl.multiple_of(j * rows, rows), count * rows), :], queries, (1, 0))
            allowed = place >= begin - j * rows
            if last:
                lane = lax.broadcasted_iota(jnp.int32, (count * rows, 2 * rows), 1) % rows
                allowed = allowed & (place <= lane + (count - 1) * rows)
            weights = jnp.where(allowed, jnp.exp2(scores * rate), 0.0)
            mass = mass + jnp.sum(weights, axis=0, keepdims=True)
            weights = weights.astype(BF)
            for part in range(count):
                total = total + dot(kv_ref[j + part, dim:, :], weights[part * rows : (part + 1) * rows], (1, 0))
            return mass, total

        state = (jnp.zeros((1, 2 * rows), F32), jnp.zeros((dim, 2 * rows), F32))
        ends = i % GROUP_FORWARD + 1
        state = lax.fori_loop(
            0, (base + i + 1 - ends) // GROUP_FORWARD, lambda j, state: tile(GROUP_FORWARD * j, state, GROUP_FORWARD, False), state
        )
        mass, total = tile(base + i + 1 - ends, state, ends, True)
        total = total / mass
        out_ref[i] = jnp.concatenate([total[:, :rows], total[:, rows:]], axis=0).astype(BF)
        mass_ref[i] = mass


def attend_back_kernel(
    rate, scale, base_ref, start_ref, q_ref, kv_ref, attn_ref, mass_ref, grad_ref,
    dq_ref, dkv_ref, key_ref, value_ref, qrow_ref, grow_ref, dk_ref, dv_ref,
):
    blocks, width, rows = q_ref.shape
    dim = width // 2
    base = base_ref[0]

    def turn(j, _):
        place = pl.ds(pl.multiple_of(j * rows, rows), rows)
        key_ref[place, :] = kv_ref[j, :dim, :].astype(F32).T.astype(BF)
        value_ref[place, :] = kv_ref[j, dim:, :].astype(F32).T.astype(BF)
        dk_ref[place, :] = jnp.zeros((rows, dim), F32)
        dv_ref[place, :] = jnp.zeros((rows, dim), F32)
        return 0

    lax.fori_loop(0, kv_ref.shape[0], turn, 0)

    def turn_rows(i, _):
        for g in range(2):
            part = slice(g * dim, (g + 1) * dim)
            qrow_ref[i, g * rows:(g + 1) * rows, :] = q_ref[i, part, :].astype(F32).T.astype(BF)
            grow_ref[i, g * rows:(g + 1) * rows, :] = grad_ref[i, part, :].astype(F32).T.astype(BF)
        return 0

    lax.fori_loop(0, blocks, turn_rows, 0)

    for i in range(blocks):
        queries = jnp.concatenate([q_ref[i, :dim, :], q_ref[i, dim:, :]], axis=1)
        grads = jnp.concatenate([grad_ref[i, :dim, :], grad_ref[i, dim:, :]], axis=1)
        attn = jnp.concatenate([attn_ref[i, :dim, :], attn_ref[i, dim:, :]], axis=1).astype(F32)
        begin = jnp.concatenate([start_ref[i], start_ref[i]], axis=1)
        delta = jnp.sum(grads.astype(F32) * attn, axis=0, keepdims=True)
        level = jnp.log(mass_ref[i]) * LOG2E

        def tile(j, dq, count, last):
            cut = pl.ds(pl.multiple_of(j * rows, rows), count * rows)
            place = lax.broadcasted_iota(jnp.int32, (count * rows, 2 * rows), 0)
            scores = dot(key_ref[cut, :], queries, (1, 0))
            allowed = place >= begin - j * rows
            if last:
                lane = lax.broadcasted_iota(jnp.int32, (count * rows, 2 * rows), 1) % rows
                allowed = allowed & (place <= lane + (count - 1) * rows)
            probs = jnp.where(allowed, jnp.exp2(scores * rate - level), 0.0)
            d_probs = dot(value_ref[cut, :], grads, (1, 0))
            d_scores = (probs * (d_probs - delta)).astype(BF)
            dv_ref[cut, :] += dot(probs.astype(BF), grow_ref[i], (1, 0))
            dk_ref[cut, :] += dot(d_scores, qrow_ref[i], (1, 0))
            for part in range(count):
                dq = dq + dot(kv_ref[j + part, :dim, :], d_scores[part * rows : (part + 1) * rows], (1, 0))
            return dq

        ends = i % GROUP_BACK + 1
        dq = lax.fori_loop(
            0, (base + i + 1 - ends) // GROUP_BACK, lambda j, dq: tile(GROUP_BACK * j, dq, GROUP_BACK, False), jnp.zeros((dim, 2 * rows), F32)
        )
        dq = tile(base + i + 1 - ends, dq, ends, True) * scale
        dq_ref[i] = jnp.concatenate([dq[:, :rows], dq[:, rows:]], axis=0).astype(BF)

    def turn_back(j, _):
        place = pl.ds(pl.multiple_of(j * rows, rows), rows)
        dkv_ref[j, :dim, :] = (dk_ref[place, :] * scale).T.astype(BF)
        dkv_ref[j, dim:, :] = dv_ref[place, :].T.astype(BF)
        return 0

    lax.fori_loop(0, kv_ref.shape[0], turn_back, 0)


def spread_kernel(strip, gate_ref, up_ref, out_ref):
    members, _, width = out_ref.shape
    local = width // 2
    wholes = [gate_ref[...].astype(F32), up_ref[...].astype(F32)]
    for d in range(members):
        firsts = [(s * members + d) * strip for s in range(local // strip)]
        out_ref[d] = jnp.concatenate(
            [whole[:, first : first + strip] for whole in wholes for first in firsts], axis=1
        ).astype(BF)


def weave_kernel(strip, in_ref, gate_ref, up_ref):
    members, _, width = in_ref.shape
    local = width // 2
    blocks = [in_ref[d].astype(F32) for d in range(members)]
    for part, ref in enumerate((gate_ref, up_ref)):
        firsts = [part * local + s * strip for s in range(local // strip)]
        ref[...] = jnp.concatenate(
            [block[:, first : first + strip] for first in firsts for block in blocks], axis=1
        )


def prepare_kernel(
    token_ref, query_ref, rest_ref, q_gain_ref, k_gain_ref, cos_ref, sin_ref, unit_ref, pre_ref, normed_ref, gain_ref
):
    dim = q_gain_ref.shape[0]
    half = dim // 2
    rows, width = token_ref.shape
    q_cols = query_ref.shape[1]
    k_cols = (rest_ref.shape[1] - 128) // 2
    kv_heads = k_cols // dim
    gains = rest_ref[:, 2 * k_cols :].astype(F32).T[:8]
    gain_ref[...] = gains
    tokens = token_ref[...].astype(F32)
    factor = lax.rsqrt(jnp.mean(tokens * tokens, axis=1, keepdims=True) + EPS)
    normed = (tokens * factor * gains[:1]).astype(BF)
    normed_ref[...] = normed
    cosine, sine = cos_ref[...], sin_ref[...]

    def turned(weight_ref, first):
        return dot(normed, weight_ref[:, first : first + 4 * dim], (1, 0)).T

    def head(pre, gain):
        scaled = pre * lax.rsqrt(jnp.mean(pre * pre, axis=0, keepdims=True) + EPS) * gain
        one, two = scaled[:half], scaled[half:]
        return jnp.concatenate([one * cosine - two * sine, two * cosine + one * sine], axis=0).astype(BF)

    for block in range(q_cols // (4 * dim)):
        pre = turned(query_ref, 4 * dim * block)
        pre_ref[4 * dim * block : 4 * dim * (block + 1), :] = pre
        for j in range(4):
            place = block * 4 + j
            unit_ref[place // 2, place % 2 * dim : (place % 2 + 1) * dim, :] = head(
                pre[j * dim : (j + 1) * dim], q_gain_ref[...]
            )
    for block in range(kv_heads // 4):
        pre = turned(rest_ref, 4 * dim * block)
        pre_ref[q_cols + 4 * dim * block : q_cols + 4 * dim * (block + 1), :] = pre
        value = turned(rest_ref, k_cols + 4 * dim * block).astype(BF)
        for j in range(4):
            part = slice(j * dim, (j + 1) * dim)
            unit_ref[block * 4 + j, 2 * dim : 3 * dim, :] = head(pre[part], k_gain_ref[...])
            unit_ref[block * 4 + j, 3 * dim :, :] = value[part]


def prepare_back_kernel(back_ref, pre_ref, q_gain_ref, k_gain_ref, cos_ref, sin_ref, out_ref, q_ref, k_ref):
    dim = q_gain_ref.shape[0]
    half = dim // 2
    kv_heads = back_ref.shape[0]
    q_cols, k_cols = 2 * kv_heads * dim, kv_heads * dim
    cosine, sine = cos_ref[...], sin_ref[...]

    def head(grad, pre, gain):
        one, two = grad[:half], grad[half:]
        scaled = jnp.concatenate([one * cosine + two * sine, two * cosine - one * sine], axis=0)
        factor = lax.rsqrt(jnp.mean(pre * pre, axis=0, keepdims=True) + EPS)
        with_gain = scaled * gain
        mean = jnp.mean(with_gain * pre, axis=0, keepdims=True)
        d_pre = factor * with_gain - pre * (factor * factor * factor * mean)
        return d_pre.astype(BF), scaled * pre * factor

    sums = [jnp.zeros(q_gain_ref.shape[:1] + back_ref.shape[2:], F32) for _ in range(2)]
    for kv in range(kv_heads):
        for g in range(3):
            first = (2 * kv + g) * dim if g < 2 else q_cols + kv * dim
            gain_ref = q_gain_ref if g < 2 else k_gain_ref
            d_pre, part = head(
                back_ref[kv, g * dim : (g + 1) * dim, :].astype(F32), pre_ref[first : first + dim, :], gain_ref[...]
            )
            out_ref[first : first + dim, :] = d_pre
            sums[g // 2] = sums[g // 2] + part
        out_ref[q_cols + k_cols + kv * dim : q_cols + k_cols + (kv + 1) * dim, :] = back_ref[kv, 3 * dim :, :]
    q_ref[...] = jnp.sum(sums[0], axis=1, keepdims=True)
    k_ref[...] = jnp.sum(sums[1], axis=1, keepdims=True)


def ffn_kernel(count, *refs):
    tokens, grads = refs[:count], refs[count : 2 * count]
    every_ref, down_ref, hn_ref, grad_ref, act_ref, d_both_ref, own_ref, other_ref = refs[2 * count :]
    at = 0
    for token_ref, one_ref in zip(tokens, grads):
        size = token_ref.shape[0]
        hn_ref[at : at + size, :] = token_ref[...]
        grad_ref[at : at + size, :] = one_ref[...]
        at += size
    line = every_ref.shape[0]
    depth = hn_ref.shape[1] // line
    local = down_ref.shape[0]
    half = own_ref.shape[0]
    step = next((size for size in (512, 256) if half % size == 0), half)
    for first in reversed(range(0, at, step)):
        cut = slice(first, first + step)
        both = sum(
            dot(hn_ref[cut, z * depth : (z + 1) * depth], every_ref[z, :depth, :], (1, 0)) for z in range(line)
        )
        d_act = dot(grad_ref[cut, :], down_ref[...], (1, 1))
        gate, up = both[:, :local], both[:, local:]
        sig = jax.nn.sigmoid(gate)
        silu = gate * sig
        act_ref[cut, :] = (silu * up).astype(BF)
        d_gate = d_act * up * (sig * (1.0 + gate * (1.0 - sig)))
        d_both = jnp.concatenate([d_gate, d_act * silu], axis=1).astype(BF)
        d_both_ref[cut, :] = d_both
        ref, place = (own_ref, first) if first < half else (other_ref, first - half)
        d_hn = [dot(d_both, every_ref[z, :depth, :], (1, 1)).astype(BF) for z in range(line)]
        ref[place : place + step, :] = jnp.concatenate(d_hn, axis=1)


def ffn_out_kernel(count, *refs):
    acts, down_ref, outs = refs[:count], refs[count], refs[count + 1 :]
    for i, act_ref in enumerate(acts):
        half = act_ref.shape[0] // 2
        for side in range(2):
            outs[2 * i + side][...] = dot(
                act_ref[side * half : (side + 1) * half, :], down_ref[...], (1, 0)
            ).astype(BF)


def ffn_weights_kernel(count, *refs):
    hns, d_boths, acts, grads = [refs[i * count : (i + 1) * count] for i in range(4)]
    out_ref = refs[4 * count]
    line, _, columns = out_ref.shape
    width, local = hns[0].shape[1], acts[0].shape[1]
    depth, strip = width // line, local // line
    for z in range(line):
        for lefts, rights, size, first in ((hns, d_boths, depth, 0), (acts, grads, strip, depth)):
            total = sum(
                dot(left[:, z * size : (z + 1) * size], right[...], (0, 0)) for left, right in zip(lefts, rights)
            )
            if total.shape[1] < columns:
                total = jnp.concatenate([total, jnp.zeros((size, columns - total.shape[1]), F32)], axis=1)
            out_ref[z, first : first + size, :] = total.astype(BF)


VMEM = pl.BlockSpec(memory_space=pltpu.VMEM)
SMEM = pl.BlockSpec(memory_space=pltpu.SMEM)
LITTLE = pl.CostEstimate(flops=1, bytes_accessed=1, transcendentals=0)
PARAMS = pltpu.CompilerParams(vmem_limit_bytes=48 * 1024 * 1024)


def attend(base, start, queries, kv, dim):
    blocks, width, rows = queries.shape
    tiles = kv.shape[0]
    pairs = blocks * (blocks + 1) // 2
    return pl.pallas_call(
        functools.partial(attend_kernel, dim ** -0.5 * LOG2E),
        out_shape=(
            jax.ShapeDtypeStruct(queries.shape, BF),
            jax.ShapeDtypeStruct((blocks, 1, 2 * rows), F32),
        ),
        in_specs=[SMEM, VMEM, VMEM, VMEM],
        out_specs=(VMEM, VMEM),
        scratch_shapes=[pltpu.VMEM((tiles * rows, dim), BF)],
        compiler_params=PARAMS,
        cost_estimate=LITTLE,
        name="attend",
    )(base, start, queries, kv)


def attend_back(base, start, queries, kv, attn, mass, grads, dim):
    blocks, width, rows = queries.shape
    tiles = kv.shape[0]
    pairs = blocks * (blocks + 1) // 2
    return pl.pallas_call(
        functools.partial(attend_back_kernel, dim ** -0.5 * LOG2E, dim ** -0.5),
        out_shape=(jax.ShapeDtypeStruct(queries.shape, BF), jax.ShapeDtypeStruct(kv.shape, BF)),
        in_specs=[SMEM] + [VMEM] * 6,
        out_specs=(VMEM, VMEM),
        scratch_shapes=[
            pltpu.VMEM((tiles * rows, dim), BF),
            pltpu.VMEM((tiles * rows, dim), BF),
            pltpu.VMEM((blocks, 2 * rows, dim), BF),
            pltpu.VMEM((blocks, 2 * rows, dim), BF),
            pltpu.VMEM((tiles * rows, dim), F32),
            pltpu.VMEM((tiles * rows, dim), F32),
        ],
        compiler_params=PARAMS,
        cost_estimate=pl.CostEstimate(flops=int(6e9), bytes_accessed=8 << 20, transcendentals=0),
        name="attend_back",
    )(base, start, queries, kv, attn, mass, grads)


def spread(gate, up, members, strip):
    rows, width = gate.shape
    return pl.pallas_call(
        functools.partial(spread_kernel, strip),
        out_shape=jax.ShapeDtypeStruct((members, rows, 2 * width // members), BF),
        in_specs=[VMEM, VMEM],
        out_specs=VMEM,
        compiler_params=PARAMS,
        name="spread",
    )(gate, up)


def weave(parts, strip):
    members, rows, width = parts.shape
    whole = jax.ShapeDtypeStruct((rows, members * width // 2), F32)
    return pl.pallas_call(
        functools.partial(weave_kernel, strip),
        out_shape=(whole, whole),
        in_specs=[VMEM],
        out_specs=(VMEM, VMEM),
        compiler_params=PARAMS,
        name="weave",
    )(parts)


def prepare_heads(tokens, w_query, w_rest, q_gain, k_gain, cosine, sine):
    rows, width = tokens.shape
    dim = q_gain.shape[0]
    q_cols = w_query.shape[1]
    k_cols = (w_rest.shape[1] - 128) // 2
    return pl.pallas_call(
        prepare_kernel,
        out_shape=(
            jax.ShapeDtypeStruct((k_cols // dim, 4 * dim, rows), BF),
            jax.ShapeDtypeStruct((q_cols + k_cols, rows), F32),
            jax.ShapeDtypeStruct((rows, width), BF),
            jax.ShapeDtypeStruct((8, width), F32),
        ),
        in_specs=[VMEM] * 7,
        out_specs=(VMEM,) * 4,
        compiler_params=PARAMS,
        cost_estimate=LITTLE,
        name="prepare",
    )(tokens, w_query, w_rest, q_gain, k_gain, cosine, sine)


def prepare_back(back, pre, q_gain, k_gain, cosine, sine):
    dim, rows = q_gain.shape[0], back.shape[2]
    return pl.pallas_call(
        prepare_back_kernel,
        out_shape=(
            jax.ShapeDtypeStruct((pre.shape[0] + back.shape[0] * dim, rows), BF),
            jax.ShapeDtypeStruct((dim, 1), F32),
            jax.ShapeDtypeStruct((dim, 1), F32),
        ),
        in_specs=[VMEM] * 6,
        out_specs=(VMEM,) * 3,
        compiler_params=PARAMS,
        cost_estimate=LITTLE,
        name="prepare_back",
    )(back, pre, q_gain, k_gain, cosine, sine)


def ffn(tokens, grads, every, down):
    total = sum(part.shape[0] for part in tokens)
    local, width = down.shape
    shapes = [(total, width), (total, width), (total, local), (total, 2 * local), (total // 2, width), (total // 2, width)]
    return pl.pallas_call(
        functools.partial(ffn_kernel, len(tokens)),
        out_shape=tuple(jax.ShapeDtypeStruct(shape, BF) for shape in shapes),
        in_specs=[VMEM] * (2 * len(tokens) + 2),
        out_specs=(VMEM,) * len(shapes),
        compiler_params=PARAMS,
        cost_estimate=LITTLE,
        name="ffn",
    )(*tokens, *grads, every, down)


def ffn_out(acts, down):
    width = down.shape[1]
    shapes = [(act.shape[0] // 2, width) for act in acts for _ in range(2)]
    outs = pl.pallas_call(
        functools.partial(ffn_out_kernel, len(acts)),
        out_shape=tuple(jax.ShapeDtypeStruct(shape, BF) for shape in shapes),
        in_specs=[VMEM] * (len(acts) + 1),
        out_specs=(VMEM,) * len(shapes),
        compiler_params=PARAMS,
        cost_estimate=pl.CostEstimate(flops=int(2.4e9), bytes_accessed=8 << 20, transcendentals=0),
        name="ffn_out",
    )(*acts, down)
    return list(zip(outs[::2], outs[1::2]))


def ffn_weights(hns, d_boths, acts, grads, every):
    line, depth, columns = every.shape
    rows = depth + acts[0].shape[1] // line
    return pl.pallas_call(
        functools.partial(ffn_weights_kernel, len(hns)),
        out_shape=jax.ShapeDtypeStruct((line, rows, columns), BF),
        in_specs=[VMEM] * (4 * len(hns)),
        out_specs=VMEM,
        compiler_params=PARAMS,
        cost_estimate=pl.CostEstimate(flops=int(7.2e9), bytes_accessed=8 << 20, transcendentals=0),
        name="ffn_weights",
    )(*hns, *d_boths, *acts, *grads)


def trade(blocks):
    return lax.all_to_all(blocks, GROUP, 0, 0, tiled=True)


def exchange(blocks):
    return lax.all_to_all(blocks, HEADS, 0, 0, tiled=True)


def on_device(
    tokens,
    attn_gain,
    q_weight,
    k_weight,
    v_weight,
    q_norm_gain,
    k_norm_gain,
    o_weight,
    ffn_gain,
    gate_weight,
    up_weight,
    down_weight,
    doc_lengths,
    cotangent,
):
    rows, width = tokens.shape[1:]
    dim = q_norm_gain.shape[0]
    line = lax.axis_size(ZAXES)
    groups = lax.axis_size("t")
    seq, pairs = lax.axis_size(SEQ), lax.axis_size(("y", "c"))
    half_pairs = pairs // 2
    here = lax.axis_index(SEQ)
    side_x, side_y, side_c = lax.axis_index("x"), lax.axis_index("y"), lax.axis_index("c")
    piece = q_weight.shape[0]
    q_cols, k_cols = q_weight.shape[1], k_weight.shape[1]
    heads, kv_heads = q_cols // dim, k_cols // dim
    blocks = kv_heads
    strip = down_weight.shape[0]
    members = lax.axis_size(GROUP)
    depth = members * piece
    local = line * strip
    whole = local // 128 * 128
    pad = 128

    lengths = doc_lengths[0]
    ends = jnp.cumsum(lengths)
    starts = ends - lengths

    def begin_of(positions):
        doc = jnp.sum((positions[:, None] >= ends[None, :]).astype(jnp.int32), axis=1)
        labels = jnp.arange(lengths.shape[0], dtype=jnp.int32)
        return jnp.sum(jnp.where(doc[:, None] == labels[None, :], starts[None, :], 0), axis=1)

    place = here * rows + jnp.arange(rows, dtype=jnp.int32)
    offset = (place - begin_of(place)).astype(F32)
    freqs = THETA ** (-jnp.arange(dim // 2, dtype=F32) * 2.0 / dim)
    angles = freqs[:, None] * offset[None, :]
    cosine, sine = jnp.cos(angles), jnp.sin(angles)
    base = lax.axis_index("t") * blocks
    span = base * rows + jnp.arange(blocks * rows, dtype=jnp.int32)
    start_rows = begin_of(span).reshape(blocks, 1, rows)
    base = base.astype(jnp.int32).reshape(1)

    gains = jnp.pad(jnp.stack([attn_gain, ffn_gain], axis=1), ((0, 0), (0, pad - 2)))

    def gather_all(array, first, second, *others):
        places = {"x": 1, "y": 2}
        array = after(gather_two(array, first, 1), *others)
        array = gather_two(array, second, places[second])
        return gather_two(array, "c", 3)

    spreaded = spread(gate_weight, up_weight, members, strip)
    mixed = trade(spreaded).reshape(depth, 2 * local)
    packed = mixed
    w_out = lax.all_gather(o_weight, SEQ + ("y", "c"), axis=0, tiled=True)
    every = lax.all_gather(packed, ZAXES, axis=0)
    first_line = gather_line(jnp.concatenate([q_weight, k_weight, v_weight, gains], axis=1))
    w_down = gather_line(after(down_weight, first_line)).reshape(local, width)
    w_query = gather_all(first_line[..., :q_cols], "x", "y", packed).reshape(width, q_cols)
    w_rest = gather_all(first_line[..., q_cols:], "y", "x", packed).reshape(width, -1)
    w_key, w_value = w_rest[:, :k_cols], w_rest[:, k_cols : 2 * k_cols]
    quarter = rows // 2

    def plane_parts(array):
        first, second = array[:quarter], array[quarter:]
        first_x, second_y = swap(first, "x"), swap(second, "y")
        far_first = swap(jnp.concatenate([first, first_x], axis=0), "y")
        far_second = swap(jnp.concatenate([second, second_y], axis=0), "x")
        parts = ((array,), (first_x, second_y), (far_first, far_second))
        return [list(part) + [swap(piece, "c") for piece in part] for part in parts]

    def plane_chip(part):
        own, other = part
        return own.astype(F32) + swap(other.astype(BF), "c").astype(F32)

    def moved(part, axis):
        return swap(part.astype(BF), axis).astype(F32)

    def plane_sum(parts, start=None):
        near, middle, far = [plane_chip(part) for part in parts]
        to_y, to_x = start((far[:rows].astype(BF), far[rows:].astype(BF)))
        from_y, from_x = moved(to_y, "y"), moved(to_x, "x")
        first = from_y[:quarter] + moved(middle[:quarter] + from_y[quarter:], "x")
        second = from_x[:quarter] + moved(middle[quarter:] + from_x[quarter:], "y")
        return near + jnp.concatenate([first, second], axis=0)

    grad_out = cotangent[0]

    inputs = tokens[0].astype(F32)
    in_factor = rms_factor(inputs)
    q_gain, k_gain = q_norm_gain.astype(F32)[:, None], k_norm_gain.astype(F32)[:, None]
    w_query = after(w_query, w_down)
    unit, pre, normed, gain_rows = prepare_heads(tokens[0], w_query, w_rest, q_gain, k_gain, cosine, sine)
    attn_gain_all, ffn_gain_all = gain_rows[0], gain_rows[1]
    unit = exchange(unit)
    grad_parts = plane_parts(after(grad_out, unit))
    unit_q, unit_kv = unit[:, : 2 * dim], unit[:, 2 * dim :]
    if groups > 1:
        unit_kv = lax.all_gather(unit_kv, "t", axis=0, tiled=True)
    unit_out, mass = attend(base, start_rows, unit_q, unit_kv, dim)
    attn_b = exchange(unit_out).reshape(heads * dim, rows)
    hidden = inputs + dot(attn_b, w_out, (0, 0))

    ffn_factor = rms_factor(hidden)
    hn = (hidden * ffn_factor * ffn_gain_all).astype(BF)
    first, second = hn[:quarter], hn[quarter:]
    first_x, second_y = swap(first, "x"), swap(second, "y")
    done = [ffn([hn, swap(hn, "c")], grad_parts[0], every, w_down)]
    first_x, second_y = lax.optimization_barrier((first_x, second_y, done[0][5]))[:2]
    far_first = swap(jnp.concatenate([first, first_x], axis=0), "y")
    far_second = swap(jnp.concatenate([second, second_y], axis=0), "x")
    done.append(ffn([first_x, second_y, swap(first_x, "c"), swap(second_y, "c")], grad_parts[1], every, w_down))
    far_first, far_second = lax.optimization_barrier((far_first, far_second, done[1][5]))[:2]
    done.append(ffn([far_first, far_second, swap(far_first, "c"), swap(far_second, "c")], grad_parts[2], every, w_down))
    hns, grad_alls, acts, d_boths = list(zip(*done))[:4]
    packed_grads = []

    def weights_after(far):
        later, boths, far = lax.optimization_barrier((acts, d_boths, far))
        packed_grads.append(ffn_weights(hns, boths, later, grad_alls, every))
        return far

    d_hn = plane_sum([part[4:] for part in done], weights_after)
    packed_grad = packed_grads[0]
    d_hn = after(d_hn, packed_grad)


    d_hidden = grad_out.astype(F32) + rms_back(hidden, ffn_factor, ffn_gain_all, d_hn)
    ffn_gain_part = jnp.sum(d_hn * hidden * ffn_factor, axis=0)
    d_branch = d_hidden.astype(BF)
    d_attn = dot(w_out, d_branch, (1, 1)).astype(BF).reshape(kv_heads, 2 * dim, rows)
    unit_grad = exchange(d_attn)

    near, middle, far = [plane_chip(part) for part in ffn_out(after(acts, d_attn), w_down)]

    def cut_core(array, side):
        return pick(array.reshape(line * 2 * half_pairs, 2, piece, -1), side, 1).reshape(line * 2 * half_pairs * piece, -1)

    def out_product(side):
        return dot(cut_core(attn_b, side), d_branch, (1, 0))

    out_kept = out_product(side_c) + swap(out_product(1 - side_c).astype(BF), "c").astype(F32)
    unit_grad = after(unit_grad, packed_grad, near, middle, far, out_kept)
    packed_grad = lax.psum_scatter(packed_grad, ZAXES, scatter_dimension=0, tiled=True)[0]
    wide_grad, down_grad = packed_grad[:depth], packed_grad[depth:, :width].astype(F32)

    from_y, from_x = moved(far[:rows], "y"), moved(far[rows:], "x")
    out_kept = out_kept.reshape(line, 2, half_pairs, piece, width)
    out_sent = swap(pick(out_kept, 1 - side_y, 2).astype(BF), "y")
    unit_dq, unit_dkv = attend_back(base, start_rows, unit_q, unit_kv, unit_out, mass, unit_grad, dim)
    if groups > 1:
        unit_dkv = lax.psum_scatter(unit_dkv.astype(F32), "t", scatter_dimension=0, tiled=True).astype(BF)
    back = exchange(jnp.concatenate([unit_dq, unit_dkv], axis=1))
    from_y, from_x, out_sent, _ = lax.optimization_barrier((from_y, from_x, out_sent, unit_dq))
    first = from_y[:quarter] + moved(middle[:quarter] + from_y[quarter:], "x")
    second = from_x[:quarter] + moved(middle[quarter:] + from_x[quarter:], "y")
    output = (hidden + near + jnp.concatenate([first, second], axis=0)).astype(BF)[None]
    out_kept = scatter_two(pick(out_kept, side_y, 2) + out_sent.astype(F32), "x", 1)
    back = after(back, packed_grad, output, out_kept)
    d_pre, q_gain_grad, k_gain_grad = prepare_back(back, pre, q_gain, k_gain, cosine, sine)

    normed_cut = normed.reshape(rows, line * 2 * half_pairs, 2, piece)

    def pre_product(side):
        left = pick(normed_cut, side, 2).reshape(rows, -1)
        return dot(left, d_pre, (0, 1))

    kept = pre_product(side_c) + swap(pre_product(1 - side_c).astype(BF), "c").astype(F32)
    d_late, wide_grad = lax.optimization_barrier((d_pre, wide_grad, kept))[:2]
    gate_grad, up_grad = weave(trade(wide_grad.reshape(members, piece, -1)), strip)
    kept = kept.reshape(line, 2, half_pairs, piece, -1)
    d_normed = (
        dot(d_late[:q_cols], w_query, (0, 1))
        + dot(d_late[q_cols : q_cols + k_cols], w_key, (0, 1))
        + dot(d_late[q_cols + k_cols :], w_value, (0, 1))
    )
    attn_gain_part = jnp.sum(d_normed * inputs * in_factor, axis=0)
    input_grad = (d_hidden + rms_back(inputs, in_factor, attn_gain_all, d_normed))[None]
    q_half, rest_half = scatter_two(kept[..., :q_cols], "x", 1), scatter_two(kept[..., q_cols:], "y", 2)
    q_half, rest_half = lax.optimization_barrier((q_half, rest_half, input_grad))[:2]
    q_half, rest_half = scatter_two(q_half, "y", 1), scatter_two(rest_half, "x", 1)
    last = jnp.concatenate([q_half, rest_half, out_kept], axis=-1)
    shares = scatter_line(last)

    count = seq * pairs
    heads_part = jnp.concatenate([q_gain_grad, k_gain_grad], axis=0).reshape(1, -1)
    small = jnp.concatenate(
        [
            attn_gain_part.reshape(count, piece), ffn_gain_part.reshape(count, piece),
            jnp.broadcast_to(heads_part, (count, 2 * dim)),
        ],
        axis=1,
    )
    small = after(small, last)
    small = jnp.sum(lax.all_to_all(small, SEQ + ("y", "c"), 0, 0, tiled=True), axis=0)
    return (
        output,
        input_grad,
        small[:piece],
        shares[:, :q_cols],
        shares[:, q_cols : q_cols + k_cols],
        shares[:, q_cols + k_cols : q_cols + 2 * k_cols],
        small[2 * piece : 2 * piece + dim],
        small[2 * piece + dim :],
        shares[:, q_cols + 2 * k_cols :],
        small[piece : 2 * piece],
        gate_grad,
        up_grad,
        down_grad,
    )


def solution(mesh):
    seq, pairs = mesh.shape["seq"], mesh.shape["dp"]

    def run(*arrays):
        kv_heads = arrays[3].shape[1] // arrays[5].shape[0]
        groups = seq // kv_heads
        fine = Mesh(mesh.devices.reshape(groups, kv_heads // 2, 2, pairs // 2, 2), ("t", "z", "x", "y", "c"))
        everywhere = ("t", "z", "x", "y", "c")
        packs = P(("y", "c"), SEQ, None)
        split, split_one = P(everywhere, None), P(everywhere)
        return jax.shard_map(
            on_device,
            mesh=fine,
            in_specs=(
                packs, split_one, split, split, split, P(), P(), split, split_one, split, split, split,
                P(("y", "c"), None), packs,
            ),
            out_specs=(
                packs, packs, split_one, split, split, split, P(), P(), split, split_one, split, split, split,
            ),
            check_vma=False,
        )(*arrays)

    return run
```
